512 devices in a mesh: gossip: 16 (over y, x_lo), fsdp: 32 (over x_hi, z, core).
Axes of the slice: x: 4 (x_hi: 2, x_lo: 2; x = x_hi * 2 + x_lo), y: 8, z: 8, core: 2. Of those that a mesh axis runs over, the one named last changes fastest.
Arguments:
- block_input: bfloat16 [16, 6144, 1024], P('gossip', 'fsdp'), may hold values from -6 to 6
- preact: bfloat16 [16, 6144, 2048], P('gossip', 'fsdp'), may hold values from -6 to 6
- cotangent: bfloat16 [16, 6144, 1024], P('gossip', 'fsdp'), may hold values from -6 to 6
- seq_ids: int32 [16, 6144], P('gossip', 'fsdp'), may hold values from 0 to 7, never falling along the last dimension, each value on 1 to 1536 neighbouring positions
- gates: float32 [16, 8, 1024], P('gossip'), may hold values from -5 to 5
- weight: float32 [16, 2048, 1024], P('gossip', 'fsdp'), may hold values from -6 to 6
- first_moment: float32 [16, 2048, 1024], P('gossip', 'fsdp'), may hold values from -4 to 4
- second_moment: float32 [16, 2048, 1024], P('gossip', 'fsdp'), may hold values from 0.1 to 4
- step: int32 [], replicated, may hold values from 0 to 63
Outputs:
- block_output: bfloat16 [16, 6144, 1024], P('gossip', 'fsdp')
- preact_grad: bfloat16 [16, 6144, 2048], P('gossip', 'fsdp')
- gate_grad: float32 [16, 8, 1024], P('gossip')
- weight_out: float32 [16, 2048, 1024], P('gossip', 'fsdp')
- first_out: float32 [16, 2048, 1024], P('gossip', 'fsdp')
- second_out: float32 [16, 2048, 1024], P('gossip', 'fsdp')
The draws below stay inside these ranges and needn't reach their ends.
Inputs may be any that keep to these rules, and one draw needn't show every extreme that they name: `seq_ids`: sequences are runs of consecutive tokens of 1 to 1536, numbered in order; one run has exactly 1536 tokens.
All inputs are finite; a program needn't handle non-finite values.
Results may differ from the reference program's by a relative error of at most 0.017.
Values may be sent and summed in bfloat16 or wider, within the bound.
A program may use at most 64 MiB of HBM per device.

```python
import math
import jax
import jax.numpy as jnp
import numpy as np
from jax import lax

D = 1024
FFW = 2048
LENGTH = 768
TOK_DEV = 192
GTOK = 6144
SEQS = 8
N_GOSSIP = 16
N_FSDP = 32


def raised(entries, own_key, source, target, shards_of, factor):
    owner, partner = [(jnp.arange(entries.shape[axis_at]) // (entries.shape[axis_at] // shards_of)).reshape([-1 if axis == axis_at else 1 for axis in range(entries.ndim)]) for axis_at in (source, target)]
    chosen = jax.random.permutation(own_key, shards_of)[partner]
    strong = (owner == chosen) | (owner == (partner + shards_of // 2) % shards_of)
    return jnp.where(strong, factor * entries, entries)


def steps_of(key, dims, cuts, low, largest):
    loudness = 1.0
    for position, shards_of in cuts:
        heights = jax.random.uniform(jax.random.fold_in(jax.random.fold_in(key, 6), position), (shards_of,), jnp.float32, low / len(cuts), largest / len(cuts))
        loudness = loudness * jnp.repeat(jnp.exp(heights), dims[position] // shards_of).reshape((-1,) + (1,) * (len(dims) - 1 - position))
    return loudness


def profile(count, total, most, lean):
    weights = [(1 << 20) // math.isqrt(grade ** lean) + 1 for grade in range(2, count + 1)]
    spare, given = total - most - (count - 1), [1] * (count - 1)
    while spare > 0:
        candidates = [i for i in range(count - 1) if given[i] < most]
        pool, remaining = sum([weights[i] for i in candidates]), spare
        for i in candidates:
            addition = min(most - given[i], max(1, remaining * weights[i] // pool), spare)
            given[i] = given[i] + addition
            spare = spare - addition
    return np.array([most] + given)


def ragged(own_key, number_of, total, reach, skew):
    if number_of == 2:
        one = jax.random.randint(own_key, (), max(1, total - reach), min(reach, total - 1) + 1)
        return jnp.stack([one, total - one])
    tallies = jnp.asarray(profile(number_of, total, reach, skew), jnp.int32)
    couples = (number_of - 1) // 2
    giver, taker = tallies[1:1 + 2 * couples:2], tallies[2:2 + 2 * couples:2]
    margin = jnp.minimum(giver - 1, reach - taker)
    shifted = jax.random.randint(jax.random.fold_in(own_key, 1), (couples,), 0, 1 << 20) % (margin + 1)
    tallies = tallies.at[1:1 + 2 * couples:2].set(giver - shifted).at[2:2 + 2 * couples:2].set(taker + shifted)
    return tallies[jax.random.permutation(jax.random.fold_in(own_key, 2), number_of)]


def gaussian(own_key, extent, deviation, most, split=(), held_as=jnp.bfloat16):
    array = deviation * jax.random.normal(own_key, extent, jnp.float32)
    if split:
        array = array * steps_of(own_key, extent, split, -0.22, 0.18)
    return jnp.clip(array, -most, most).astype(held_as)


def heavy_noise(key, dims, spread, reach, cuts, heavy, held_as=jnp.bfloat16):
    array = spread * jax.random.normal(key, dims, jnp.float32)
    if cuts:
        array = array * steps_of(key, dims, cuts, -0.22, 0.18)
    return jnp.clip(raised(array, jax.random.fold_in(key, 3), *heavy), -reach, reach).astype(held_as)


def setup_inputs(seed: int = 0) -> dict:
    key_of = jax.random.split(jax.random.key(seed), 10)
    return {
        "block_input": gaussian(key_of[0], (N_GOSSIP, GTOK, D), 1.0, 6.0, ((0, 16), (1, 32))),
        "preact": heavy_noise(key_of[1], (N_GOSSIP, GTOK, FFW), 1.0, 6.0, ((0, 16), (1, 32)), (1, 2, 32, 2.75)),
        "cotangent": gaussian(key_of[2], (N_GOSSIP, GTOK, D), 1.0, 6.0, ((0, 16), (1, 32))),
        "seq_ids": jax.vmap(lambda own: jnp.searchsorted(jnp.cumsum(ragged(own, SEQS, GTOK, 2 * LENGTH, 0)), jnp.arange(GTOK), side="right"))(jax.random.split(key_of[3], N_GOSSIP)).reshape((N_GOSSIP, GTOK)).astype(jnp.int32),
        "gates": gaussian(key_of[4], (N_GOSSIP, SEQS, D), 1.0, 5.0, ((0, 16),), jnp.float32),
        "weight": gaussian(key_of[5], (N_GOSSIP, FFW, D), 1.0, 6.0, ((0, 16), (1, 32)), jnp.float32),
        "first_moment": gaussian(key_of[6], (N_GOSSIP, FFW, D), 0.5, 4.0, ((0, 16), (1, 32)), jnp.float32),
        "second_moment": jnp.clip(jnp.exp(math.log(4.0) - 3.6888794 * jax.random.uniform(key_of[7], (N_GOSSIP, FFW, D), jnp.float32) ** steps_of(key_of[7], (N_GOSSIP, FFW, D), ((0, 16), (1, 32)), -0.2, 0.2)), 0.1, 4.0),
        "step": jax.random.randint(key_of[8], (), 0, 64).astype(jnp.int32),
    }


def gelu_parts(values):
    inner = 0.7978845608 * (values + 0.044715 * values * values * values)
    tangent = jnp.tanh(inner)
    activated = 0.5 * values * (1.0 + tangent)
    slope = 0.5 * (1.0 + tangent) + 0.5 * values * (1.0 - tangent * tangent) * 0.7978845608 * (1.0 + 3.0 * 0.044715 * values * values)
    return (activated, slope)

def reference(block_input, preact, cotangent, seq_ids, gates, weight, first_moment, second_moment, step):
    scaling = FFW ** (-0.5)
    outputs, pre_grads, gate_grads, stepped_all, firsts, seconds = ([], [], [], [], [], [])
    counter = (step + 1).astype(jnp.float32)
    corr_first = 1.0 - jnp.power(jnp.float32(0.9), counter)
    corr_second = 1.0 - jnp.power(jnp.float32(0.999), counter)
    for replica in range(N_GOSSIP):
        pre_vals = preact[replica].astype(jnp.float32)
        activated, slope = gelu_parts(pre_vals)
        hidden = activated.astype(jnp.bfloat16)
        weight_low = weight[replica].astype(jnp.bfloat16)
        projected = jnp.dot(hidden, weight_low, preferred_element_type=jnp.float32) * scaling
        token_gate = gates[replica][seq_ids[replica]]
        outputs.append((block_input[replica].astype(jnp.float32) + token_gate * projected).astype(jnp.bfloat16))
        cot_vals = cotangent[replica].astype(jnp.float32)
        scaled_cot = (token_gate * cot_vals).astype(jnp.bfloat16)
        gate_grads.append(jax.ops.segment_sum(cot_vals * projected, seq_ids[replica], num_segments=SEQS))
        hidden_blocks = hidden.astype(jnp.float32).reshape(N_FSDP, TOK_DEV, FFW)
        cot_blocks = scaled_cot.astype(jnp.float32).reshape(N_FSDP, TOK_DEV, D)
        partial_terms = jnp.einsum('jtf,jtd->jfd', hidden_blocks, cot_blocks) * scaling
        rounded = lax.optimization_barrier(partial_terms.astype(jnp.bfloat16))
        grad = lax.optimization_barrier(jnp.sum(rounded.astype(jnp.float32), axis=0))
        hidden_grad = jnp.dot(scaled_cot, weight_low.T, preferred_element_type=jnp.float32) * scaling
        pre_grads.append((hidden_grad * slope).astype(jnp.bfloat16))
        first_new = 0.9 * first_moment[replica] + 0.1 * grad
        second_new = 0.999 * second_moment[replica] + 0.001 * grad * grad
        update = first_new / corr_first / (jnp.sqrt(second_new / corr_second) + 1e-08)
        stepped_all.append(weight[replica] - 0.01 * (update + 0.1 * weight[replica]))
        firsts.append(first_new)
        seconds.append(second_new)
    stepped = jnp.stack(stepped_all)
    levels = N_GOSSIP.bit_length() - 1
    distance = jnp.left_shift(jnp.int32(1), (step % levels).astype(jnp.int32))
    sources = ((jnp.arange(N_GOSSIP, dtype=jnp.int32) - distance) % N_GOSSIP).astype(jnp.int32)
    weight_out = 0.5 * (stepped + stepped[sources])
    return (jnp.stack(outputs), jnp.stack(pre_grads), jnp.stack(gate_grads), weight_out, jnp.stack(firsts), jnp.stack(seconds))
```

```python
import functools

import jax
import jax.numpy as jnp
from jax import lax
from jax.experimental import pallas as pl
from jax.experimental.pallas import tpu as pltpu
from jax.sharding import PartitionSpec as P

MESH = pl.DeviceIdType.MESH
BF16, F32 = jnp.bfloat16, jnp.float32

TOK, FFW, D, SEQS = 192, 2048, 1024, 8
ROWS, HALF = 64, 512
NZ = 8
N_GOSSIP = 16

GATHER_HOPS = ((4, 3), (3, 4), (4, 3))
SUM_HOPS = ((3, 4), (4, 3), (3, 4))
X_ORDER = (4, 3, -3, 2, -2, 1, -1, 0)
PEERS = tuple(range(1, NZ))


def kernel(
    shift,
    step_ref, seq_ref, gates_ref, w_h, m1_h, m2_h, pre_h, cot_h, bi_h,
    bo_h, pg_h, gg_h, wo_h, fo_h, so_h,
    w_v, m1_v, m2_v, pre_v, cot_v, bi_v,
    wg, hid, slope_v, ht, hts, sc, scs, tg_v,
    part, rz, rx, rxa,
    gl, gl_r, gx, gx_r, gz, gg_o, gg_r,
    st_v, st_s, st_r, bo_v, pg_v, gg_v, wo_v, fo_v, so_v,
    lsem, osem,
    agz_s, agz_r, agx_s, agx_r, ags_s, ags_r,
    tok_s, tok_r, rsz_s, rsz_r, rsx_s, rsx_r, gg_ss, gg_rs, go_s, go_r,
):
    g = lax.axis_index("gossip")
    f = lax.axis_index("fsdp")
    xh = lax.div(f, 16)
    z = lax.rem(lax.div(f, 2), NZ)
    c = lax.rem(f, 2)
    xo, co = 1 - xh, 1 - c
    scaling = FFW ** -0.5

    def zat(k):
        return lax.rem(z + (k % NZ), NZ)

    def dev(xx, zz, cc):
        return {"fsdp": xx * 16 + zz * 2 + cc}

    znext = (dev(xh, zat(1), c), dev(xh, zat(-1), c))
    xdev, sdev = dev(xo, z, c), dev(xh, z, co)
    up = {"gossip": lax.rem(g + shift, N_GOSSIP)}
    down = {"gossip": lax.rem(g + N_GOSSIP - shift, N_GOSSIP)}

    sent = []

    def describe(src, dst, ssem, rsem, to):
        return pltpu.make_async_remote_copy(
            src_ref=src, dst_ref=dst, send_sem=ssem, recv_sem=rsem, device_id=to, device_id_type=MESH
        )

    def send(src, dst, ssem, rsem, to):
        copy = describe(src, dst, ssem, rsem, to)
        copy.start()
        sent.append(copy)

    def arrive(dst, ssem, rsem, to):
        describe(dst, dst, ssem, rsem, to).wait_recv()

    loads = []
    for i, (src, dst) in enumerate(
        ((w_h, w_v), (cot_h, cot_v), (pre_h, pre_v), (bi_h, bi_v), (m1_h, m1_v), (m2_h, m2_v))
    ):
        copy = pltpu.make_async_copy(src, dst, lsem.at[i])
        copy.start()
        loads.append(copy)
    load_w, load_cot, load_pre, load_bi, load_m1, load_m2 = loads

    barrier = pltpu.get_barrier_semaphore()
    greeted = [xdev, sdev, down] + [dev(xh, zat(k), c) for k in PEERS]
    for to in greeted:
        pl.semaphore_signal(barrier, inc=1, device_id=to, device_id_type=MESH)

    def place(h, xx, zz, cc):
        return wg.at[h, xx * 16 + zz * 2 + cc]

    load_w.wait()
    for h in range(2):
        wg[h, f] = w_v[:, h * HALF:(h + 1) * HALF].astype(BF16)
    pl.semaphore_wait(barrier, len(greeted))

    def gather_x(h, j, zz):
        block = place(h, xh, zz, c)
        i = 9 * h + j
        send(block, block, agx_s.at[i], agx_r.at[i], xdev)

    def gather_x_arrive(h, j, zz):
        i = 9 * h + j
        arrive(place(h, xo, zz, c), agx_s.at[i], agx_r.at[i], xdev)

    def gather_s(h, rel, j, xx, zz):
        block = place(h, xx, zz, c)
        i = 18 * h + 9 * rel + j
        send(block, block, ags_s.at[i], ags_r.at[i], sdev)

    def gather_z(stream, way, s, h, xx, zz):
        block = place(h, xx, zz, c)
        i = 8 * stream + 4 * way + s - 1
        send(block, block, agz_s.at[i], agz_r.at[i], znext[way])

    stream_of = ((0, xh, 0), (0, xo, 1), (1, xh, 0))

    def gather_step(stream, s):
        h, xx, rel = stream_of[stream]
        for way in range(2):
            hops = GATHER_HOPS[stream][way]
            if s > hops:
                continue
            zz = zat(-s if way == 0 else s)
            i = 8 * stream + 4 * way + s - 1
            arrive(place(h, xx, zz, c), agz_s.at[i], agz_r.at[i], znext[way])
            if s < hops:
                gather_z(stream, way, s + 1, h, xx, zz)
            j = 1 + 4 * way + s - 1
            if stream == 2:
                gather_x(1, j, zz)
            gather_s(h, rel, j, xx, zz)

    gather_x(0, 0, z)
    for way in range(2):
        gather_z(0, way, 1, 0, xh, z)
    for way in range(2):
        gather_z(2, way, 1, 1, xh, z)
    gather_x(1, 0, z)
    for h in range(2):
        gather_s(h, 0, 0, xh, z)

    onehot = lax.broadcasted_iota(jnp.int32, (SEQS, TOK), 0) == jnp.broadcast_to(seq_ref[...], (SEQS, TOK))
    onehot = jnp.where(onehot, 1.0, 0.0).astype(F32)
    gates = gates_ref[...]
    hi = gates.astype(BF16).astype(F32)
    mid = (gates - hi).astype(BF16).astype(F32)
    low = (gates - hi - mid).astype(BF16).astype(F32)
    select = jnp.concatenate([onehot] * 3, axis=0).T.astype(BF16)
    tg_v[...] = jnp.dot(
        select, jnp.concatenate([hi, mid, low], axis=0).astype(BF16), preferred_element_type=F32
    )
    load_cot.wait()
    for h in range(2):
        cols = slice(h * HALF, (h + 1) * HALF)
        sc[h] = (tg_v[:, cols] * cot_v[:, cols].astype(F32)).astype(BF16)
    send(sc, scs, tok_s.at[0], tok_r.at[0], sdev)

    gather_x_arrive(0, 0, z)
    for way in range(2):
        gather_z(1, way, 1, 0, xo, z)
    gather_s(0, 1, 0, xo, z)

    load_pre.wait()

    def gelu(xx, j):
        cols = pl.ds(pl.multiple_of((xx * NZ + j) * 128, 128), 128)
        u = pre_v[:, cols].astype(F32)
        sq = u * u
        th = jnp.tanh(0.7978845608 * (u + 0.044715 * sq * u))
        slope_v[:, cols] = 0.5 * (1.0 + th) + 0.5 * u * (1.0 - th * th) * 0.7978845608 * (
            1.0 + 3.0 * 0.044715 * sq
        )
        low_hidden = (0.5 * u * (1.0 + th)).astype(BF16)
        hid[:, cols] = low_hidden
        ht[xx, j] = low_hidden.T.reshape(2, ROWS, TOK)

    def gelu_run(xx):
        @pl.loop(0, NZ)
        def _(j):
            gelu(xx, j)

    gelu_run(xo)
    send(ht.at[xo, :, co], hts.at[xo], tok_s.at[1], tok_r.at[1], sdev)
    gather_step(0, 1)
    gather_step(2, 1)
    gelu_run(xh)
    send(ht.at[xh, :, co], hts.at[xh], tok_s.at[2], tok_r.at[2], sdev)
    gather_step(1, 1)
    gather_step(0, 2)
    gather_step(2, 2)

    def grad(h, xx):
        own = ht[xx, :, c].reshape(NZ * ROWS, TOK)
        other = hts[xx].reshape(NZ * ROWS, TOK)
        total = jnp.dot(own, sc[h], preferred_element_type=F32)
        total += jnp.dot(other, scs[h], preferred_element_type=F32)
        part[h, xx] = (total * scaling).astype(BF16).reshape(NZ, ROWS, HALF)

    slots = rz.at

    def sum_step(stream, s):
        h, xx = ((0, xo), (0, xh), (1, xh))[stream]
        for way in range(2):
            hops = SUM_HOPS[stream][way]
            if s > hops:
                continue
            off = (hops - s + 1) * (1 if way == 0 else -1)
            zz = zat(off)
            block = part.at[h, xx, zz]
            i = 8 * stream + 4 * way + s - 1
            if s > 1 or stream == 2:
                value = block[...].astype(F32)
                if stream == 2:
                    jx = X_ORDER.index(4 if off == -4 else off)
                    arrive(rx.at[jx], rsx_s.at[jx], rsx_r.at[jx], xdev)
                    value += rx[jx].astype(F32)
                if s > 1:
                    arrive(slots[i - 1], rsz_s.at[i - 1], rsz_r.at[i - 1], znext[way])
                    value += rz[i - 1].astype(F32)
                block[...] = value.astype(BF16)
            send(block, slots[i], rsz_s.at[i], rsz_r.at[i], znext[way])

    def sum_last(stream):
        h, xx = ((0, xo), (0, xh), (1, xh))[stream]
        value = part[h, xx, z].astype(F32)
        if stream == 2:
            arrive(rx.at[7], rsx_s.at[7], rsx_r.at[7], xdev)
            value += rx[7].astype(F32)
        for way in range(2):
            i = 8 * stream + 4 * way + SUM_HOPS[stream][way] - 1
            arrive(slots[i], rsz_s.at[i], rsz_r.at[i], znext[way])
            value += rz[i].astype(F32)
        return value

    arrive(scs, tok_s.at[0], tok_r.at[0], sdev)
    arrive(hts.at[xo], tok_s.at[1], tok_r.at[1], sdev)
    grad(1, xo)
    for j, off in enumerate(X_ORDER):
        send(part.at[1, xo, zat(off)], rx.at[j], rsx_s.at[j], rsx_r.at[j], xdev)
    grad(0, xo)
    sum_step(0, 1)
    gather_step(1, 2)
    arrive(hts.at[xh], tok_s.at[2], tok_r.at[2], sdev)
    grad(0, xh)
    sum_step(1, 1)
    gather_step(0, 3)
    gather_step(2, 3)
    grad(1, xh)
    gather_step(1, 3)
    sum_step(0, 2)
    sum_step(1, 2)
    sum_step(2, 1)
    for stream in range(3):
        gather_step(stream, 4)
    sum_step(0, 3)
    sum_step(1, 3)
    sum_step(2, 2)

    def offsets(stream):
        yield 0, 0
        for way in range(2):
            for s in range(1, GATHER_HOPS[stream][way] + 1):
                yield 1 + 4 * way + s - 1, (-s if way == 0 else s)

    def gather_rest(h):
        if h == 1:
            for j, off in offsets(2):
                gather_x_arrive(1, j, zat(off))
                gather_s(1, 1, j, xo, zat(off))
        for rel, xx, stream in ((0, xh, 2 * h), (1, xo, 1 + h)):
            for j, off in offsets(stream):
                i = 18 * h + 9 * rel + j
                arrive(place(h, xx, zat(off), co), ags_s.at[i], ags_r.at[i], sdev)

    outs = []

    def out(src, dst):
        copy = pltpu.make_async_copy(src, dst, osem.at[len(outs)])
        copy.start()
        outs.append(copy)

    def forward(h):
        cols = slice(h * HALF, (h + 1) * HALF)
        projected = jnp.dot(hid[...], wg[h].reshape(FFW, HALF), preferred_element_type=F32) * scaling
        bo_v[:, cols] = (bi_v[:, cols].astype(F32) + tg_v[:, cols] * projected).astype(BF16)
        out(bo_v.at[:, cols], bo_h.at[:, cols])
        product = cot_v[:, cols].astype(F32) * projected
        hi = product.astype(BF16)
        low = (product - hi.astype(F32)).astype(BF16)
        pick = onehot.astype(BF16)
        gl[h] = jnp.dot(pick, hi, preferred_element_type=F32) + jnp.dot(pick, low, preferred_element_type=F32)

    load_bi.wait()
    gather_rest(0)
    forward(0)
    sum_step(0, 4)
    sum_step(1, 4)
    sum_step(2, 3)
    gather_rest(1)
    forward(1)

    send(gl.at[co], gl_r, gg_ss.at[0], gg_rs.at[0], sdev)
    sum_step(2, 4)

    def backward(q):
        rows = wg.at[0, pl.ds(q * 8, 8)][...].reshape(HALF, HALF), wg.at[1, pl.ds(q * 8, 8)][...].reshape(HALF, HALF)
        cols = slice(q * HALF, (q + 1) * HALF)
        dims = (((1,), (1,)), ((), ()))
        total = lax.dot_general(sc[0], rows[0], dims, preferred_element_type=F32)
        total += lax.dot_general(sc[1], rows[1], dims, preferred_element_type=F32)
        pg_v[:, cols] = (total * scaling * slope_v[:, cols]).astype(BF16)
        out(pg_v.at[:, cols], pg_h.at[:, cols])

    backward(0)
    arrive(gl_r, gg_ss.at[0], gg_rs.at[0], sdev)
    chip = gl[c] + gl_r[...]
    gx[...] = jnp.concatenate([chip[:, :256], chip[:, 256:]], axis=0).astype(BF16)
    send(gx, gx_r, gg_ss.at[1], gg_rs.at[1], xdev)
    value = sum_last(0)
    part[0, xo, z] = value.astype(BF16)
    send(part.at[0, xo, z], rxa, rsx_s.at[8], rsx_r.at[8], xdev)
    backward(1)
    arrive(gx_r, gg_ss.at[1], gg_rs.at[1], xdev)
    gz[z] = (gx[...].astype(F32) + gx_r[...].astype(F32)).astype(BF16)
    for k in PEERS:
        send(gz.at[z], gz.at[z], gg_ss.at[1 + k], gg_rs.at[1 + k], dev(xh, zat(k), c))

    counter = jnp.full((1, HALF), step_ref[0, 0] + 1, jnp.int32)

    def power(base):
        total, factor = jnp.ones((1, HALF), F32), jnp.full((1, HALF), base, F32)
        for bit in range(7):
            on = jnp.bitwise_and(jnp.right_shift(counter, bit), 1) == 1
            total = jnp.where(on, total * factor, total)
            factor = factor * factor
        return total

    corr_first, corr_second = 1.0 - power(0.9), 1.0 - power(0.999)

    def update(h, total):
        cols = slice(h * HALF, (h + 1) * HALF)
        first = 0.9 * m1_v[:, cols] + 0.1 * total
        second = 0.999 * m2_v[:, cols] + 0.001 * total * total
        fo_v[:, cols], so_v[:, cols] = first, second
        ratio = first / corr_first / (jnp.sqrt(second / corr_second) + 1e-08)
        master = w_v[:, cols]
        stepped = master - 0.01 * (ratio + 0.1 * master)
        st_v[h] = stepped
        st_s[h] = stepped.astype(BF16)
        send(st_s.at[h], st_r.at[h], go_s.at[h], go_r.at[h], up)
        out(fo_v.at[:, cols], fo_h.at[:, cols])
        out(so_v.at[:, cols], so_h.at[:, cols])

    load_m1.wait()
    load_m2.wait()
    update(1, sum_last(2))
    value = sum_last(1)
    arrive(rxa, rsx_s.at[8], rsx_r.at[8], xdev)
    update(0, value + rxa[...].astype(F32))
    backward(2)
    backward(3)

    for k in PEERS:
        zz = zat(-k)
        arrive(gz.at[zz], gg_ss.at[1 + k], gg_rs.at[1 + k], dev(xh, zz, c))
    total = gz[0].astype(F32)
    for zz in range(1, NZ):
        total += gz[zz].astype(F32)
    gg_o[...] = jnp.concatenate([total[:SEQS], total[SEQS:]], axis=1)
    send(gg_o, gg_r, gg_ss.at[9], gg_rs.at[9], sdev)

    def finish(h):
        cols = slice(h * HALF, (h + 1) * HALF)
        arrive(st_r.at[h], go_s.at[h], go_r.at[h], up)
        wo_v[:, cols] = 0.5 * (st_v[h] + st_r[h].astype(F32))
        out(wo_v.at[:, cols], wo_h.at[:, cols])

    finish(1)
    arrive(gg_r, gg_ss.at[9], gg_rs.at[9], sdev)
    gg_v[c] = gg_o[...]
    gg_v[co] = gg_r[...]
    for h in range(2):
        out(gg_v.at[h], gg_h.at[:, h * HALF:(h + 1) * HALF])
    finish(0)

    for copy in sent:
        copy.wait_send()
    for copy in outs:
        copy.wait()


def fused(shift, place, step, seq_ids, gates, *large):
    vmem, hbm = pltpu.VMEM, pl.ANY
    dma = pltpu.SemaphoreType.DMA
    return pl.pallas_call(
        functools.partial(kernel, shift),
        out_shape=(
            jax.ShapeDtypeStruct((TOK, D), BF16),
            jax.ShapeDtypeStruct((TOK, FFW), BF16),
            jax.ShapeDtypeStruct((SEQS, D), F32),
            jax.ShapeDtypeStruct((ROWS, D), F32),
            jax.ShapeDtypeStruct((ROWS, D), F32),
            jax.ShapeDtypeStruct((ROWS, D), F32),
        ),
        in_specs=[
            pl.BlockSpec(memory_space=pltpu.SMEM),
            pl.BlockSpec(memory_space=vmem),
            pl.BlockSpec(memory_space=vmem),
        ]
        + [pl.BlockSpec(memory_space=hbm)] * 6,
        out_specs=[pl.BlockSpec(memory_space=hbm)] * 6,
        scratch_shapes=[
            vmem((ROWS, D), F32), vmem((ROWS, D), F32), vmem((ROWS, D), F32),
            vmem((TOK, FFW), BF16), vmem((TOK, D), BF16), vmem((TOK, D), BF16),
            vmem((2, 32, ROWS, HALF), BF16),
            vmem((TOK, FFW), BF16), vmem((TOK, FFW), F32),
            vmem((2, NZ, 2, ROWS, TOK), BF16), vmem((2, NZ, ROWS, TOK), BF16),
            vmem((2, TOK, HALF), BF16), vmem((2, TOK, HALF), BF16), vmem((TOK, D), F32),
            vmem((2, 2, NZ, ROWS, HALF), BF16), vmem((24, ROWS, HALF), BF16),
            vmem((NZ, ROWS, HALF), BF16), vmem((ROWS, HALF), BF16),
            vmem((2, SEQS, HALF), F32), vmem((SEQS, HALF), F32),
            vmem((2 * SEQS, HALF // 2), BF16), vmem((2 * SEQS, HALF // 2), BF16),
            vmem((NZ, 2 * SEQS, HALF // 2), BF16), vmem((SEQS, HALF), F32), vmem((SEQS, HALF), F32),
            vmem((2, ROWS, HALF), F32), vmem((2, ROWS, HALF), BF16), vmem((2, ROWS, HALF), BF16),
            vmem((TOK, D), BF16), vmem((TOK, FFW), BF16), vmem((2, SEQS, HALF), F32),
            vmem((ROWS, D), F32), vmem((ROWS, D), F32), vmem((ROWS, D), F32),
            dma((6,)), dma((14,)),
            dma((24,)), dma((24,)), dma((18,)), dma((18,)), dma((36,)), dma((36,)),
            dma((3,)), dma((3,)), dma((24,)), dma((24,)), dma((9,)), dma((9,)),
            dma((10,)), dma((10,)), dma((2,)), dma((2,)),
        ],
        compiler_params=pltpu.CompilerParams(
            collective_id=place, has_side_effects=True, vmem_limit_bytes=48 << 20
        ),
        name="block_step",
    )(step, seq_ids, gates, *large)


def on_device(
    block_input, preact, cotangent, seq_ids, gates, weight, first_moment, second_moment, step
):
    operands = (
        step.reshape(1, 1), seq_ids, gates[0], weight[0], first_moment[0], second_moment[0],
        preact[0], cotangent[0], block_input[0],
    )
    levels = N_GOSSIP.bit_length() - 1
    branches = [functools.partial(fused, 1 << level, level) for level in range(levels)]
    results = lax.switch(lax.rem(step, levels), branches, *operands)
    return tuple(array[None] for array in results)


def solution(mesh):
    split, whole = P("gossip", "fsdp", None), P("gossip", None, None)
    return jax.shard_map(
        on_device,
        mesh=mesh,
        in_specs=(split, split, split, P("gossip", "fsdp"), whole, split, split, split, P()),
        out_specs=(split, split, whole, split, split, split),
        check_vma=False,
    )
```

```python
import functools

import jax
import jax.numpy as jnp
from jax import lax
from jax.experimental import pallas as pl
from jax.experimental.pallas import tpu as pltpu
from jax.sharding import PartitionSpec as P

MESH = pl.DeviceIdType.MESH
BF16, F32 = jnp.bfloat16, jnp.float32

TOK, FFW, D, SEQS = 192, 2048, 1024, 8
ROWS, HALF = 64, 512
NZ = 8
N_GOSSIP = 16

GATHER_HOPS = ((4, 3), (3, 4), (4, 3))
SUM_HOPS = ((3, 4), (4, 3), (3, 4))
X_ORDER = (4, 3, -3, 2, -2, 1, -1, 0)
PEERS = tuple(range(1, NZ))
SCHEDULE = (
    ("own", 1, 0), ("own", 1, 1), ("own", 0, 2), ("own", 0, 1), ("gelu", 0), ("own", 0, 0), ("own", 1, 2), ("tg",), ("gelu", 1),
    ("gz", 2, 0, 1), ("gz", 2, 1, 1), ("gx", 0, 0), ("grad", 1, 1), ("xs", 0), ("xs", 1), ("grad", 0, 0), ("gz", 0, 0, 1),
    ("grad", 0, 1), ("grad", 1, 0), ("xs", 2), ("xs", 4), ("rs", 0, 1, 1), ("gz", 0, 1, 1), ("gz", 2, 0, 2), ("own", 0, 3),
    ("gz", 2, 1, 2), ("rs", 1, 0, 1), ("gz", 0, 0, 2), ("rs", 0, 1, 2), ("gz", 1, 0, 1), ("xs", 6), ("gz", 2, 0, 3),
    ("rs", 2, 0, 1), ("rs", 0, 0, 1), ("xs", 3), ("gx", 1, 1), ("rs", 2, 1, 1), ("gx", 1, 0), ("rs", 1, 1, 1), ("gz", 2, 1, 3),
    ("gz", 1, 1, 1), ("gz", 1, 0, 2), ("gz", 0, 1, 2), ("rs", 2, 1, 2), ("gz", 0, 0, 3), ("gz", 2, 0, 4), ("xs", 5),
    ("gx", 1, 2), ("gz", 1, 1, 2), ("gz", 0, 1, 3), ("rs", 0, 1, 3), ("rs", 1, 0, 2), ("gx", 1, 6), ("rs", 0, 0, 2), ("xs", 7),
    ("gx", 1, 3), ("rs", 1, 1, 2), ("gz", 1, 0, 3), ("own", 1, 3), ("rs", 2, 0, 2), ("rs", 2, 1, 3), ("gz", 1, 1, 3),
    ("gx", 1, 7), ("gx", 1, 5), ("gx", 1, 4), ("rs", 0, 1, 4), ("rs", 1, 0, 3), ("rs", 0, 0, 3), ("rs", 2, 1, 4),
    ("rs", 2, 0, 3), ("rs", 1, 1, 3), ("fwd", 1), ("gz", 0, 0, 4), ("gz", 1, 1, 4), ("last", 0), ("rs", 1, 0, 4), ("fwd", 0),
    ("last", 2), ("gate", 0), ("gate", 1), ("last", 1), ("gate", 2), ("bwd", 2), ("gate", 3), ("bwd", 1), ("bwd", 0),
    ("bwd", 3), ("fin", 1), ("gate", 4), ("fin", 0),
)


def kernel(
    shift,
    step_h, seq_h, gates_h, w_h, m1_h, m2_h, pre_h, cot_h, bi_h,
    bo_v, pg_v, gg_v, wo_v, fo_v, so_v,
    step_ref, seq_ref, gates_ref, w_v, m1_v, m2_v, pre_v, cot_v, bi_v,
    wg, hid, slope_v, ht, hts, sc, scs, tg_v,
    part, rz, rx, rxa,
    gl, gl_r, gx, gx_r, gz, gg_o, gg_r,
    st_v, st_s, st_r,
    lsem,
    agz_s, agz_r, agx_s, agx_r, ags_s, ags_r,
    tok_s, tok_r, rsz_s, rsz_r, rsx_s, rsx_r, gg_ss, gg_rs, go_s, go_r,
):
    g = lax.axis_index("gossip")
    f = lax.axis_index("fsdp")
    xh = lax.div(f, 16)
    z = lax.rem(lax.div(f, 2), NZ)
    c = lax.rem(f, 2)
    xo, co = 1 - xh, 1 - c
    scaling = FFW ** -0.5

    def zat(k):
        return lax.rem(z + (k % NZ), NZ)

    def dev(xx, zz, cc):
        return {"fsdp": xx * 16 + zz * 2 + cc}

    znext = (dev(xh, zat(1), c), dev(xh, zat(-1), c))
    xdev, sdev = dev(xo, z, c), dev(xh, z, co)
    up = {"gossip": lax.rem(g + shift, N_GOSSIP)}
    down = {"gossip": lax.rem(g + N_GOSSIP - shift, N_GOSSIP)}

    sent = []

    def describe(src, dst, ssem, rsem, to):
        return pltpu.make_async_remote_copy(
            src_ref=src, dst_ref=dst, send_sem=ssem, recv_sem=rsem, device_id=to, device_id_type=MESH
        )

    def send(src, dst, ssem, rsem, to):
        copy = describe(src, dst, ssem, rsem, to)
        copy.start()
        sent.append(copy)

    def arrive(dst, ssem, rsem, to):
        describe(dst, dst, ssem, rsem, to).wait_recv()

    loads = {}

    def load(name, src, dst):
        loads[name] = pltpu.make_async_copy(src, dst, lsem.at[len(loads)])
        loads[name].start()

    def need(*wanted):
        for name in wanted:
            if name in loads:
                loads.pop(name).wait()
                waited.append(name)

    waited = []
    load("w", w_h, w_v)
    barrier = pltpu.get_barrier_semaphore()
    greeted = [xdev, sdev, down] + [dev(xh, zat(k), c) for k in PEERS]
    for to in greeted:
        pl.semaphore_signal(barrier, inc=1, device_id=to, device_id_type=MESH)
    rest = (
        ("seq", seq_h, seq_ref), ("gates", gates_h, gates_ref), ("cot", cot_h, cot_v), ("pre", pre_h, pre_v),
        ("bi", bi_h, bi_v), ("step", step_h, step_ref), ("m1", m1_h, m1_v), ("m2", m2_h, m2_v),
    )
    for item in rest:
        load(*item)

    def place(h, xx, zz, cc):
        return wg.at[h, xx * 16 + zz * 2 + cc]

    need("w")
    for h in range(2):
        wg[h, f] = w_v[:, h * HALF:(h + 1) * HALF].astype(BF16)
    pl.semaphore_wait(barrier, len(greeted))

    def send_x(h, j, zz):
        block = place(h, xh, zz, c)
        i = 9 * h + j
        send(block, block, agx_s.at[i], agx_r.at[i], xdev)

    def send_s(h, rel, j, xx, zz):
        block = place(h, xx, zz, c)
        i = 18 * h + 9 * rel + j
        send(block, block, ags_s.at[i], ags_r.at[i], sdev)

    def send_z(stream, way, s, h, xx, zz):
        block = place(h, xx, zz, c)
        i = 8 * stream + 4 * way + s - 1
        send(block, block, agz_s.at[i], agz_r.at[i], znext[way])

    def own(h, link):
        if link < 2:
            send_z(2 * h, link, 1, h, xh, z)
        elif link == 2:
            send_x(h, 0, z)
        else:
            send_s(h, 0, 0, xh, z)

    def pass_z(stream, way, s):
        h, xx, rel = ((0, xh, 0), (0, xo, 1), (1, xh, 0))[stream]
        zz = zat(-s if way == 0 else s)
        i = 8 * stream + 4 * way + s - 1
        arrive(place(h, xx, zz, c), agz_s.at[i], agz_r.at[i], znext[way])
        if s < GATHER_HOPS[stream][way]:
            send_z(stream, way, s + 1, h, xx, zz)
        j = 4 * way + s
        if stream == 2:
            send_x(1, j, zz)
        send_s(h, rel, j, xx, zz)

    def offset(j):
        return 0 if j == 0 else -j if j <= 4 else j - 4

    def pass_x(h, j):
        zz = zat(offset(j))
        i = 9 * h + j
        arrive(place(h, xo, zz, c), agx_s.at[i], agx_r.at[i], xdev)
        if h == 0:
            for way in range(2):
                send_z(1, way, 1, 0, xo, zz)
        send_s(h, 1, j, xo, zz)

    def onehot():
        ids = jnp.broadcast_to(seq_ref[...], (SEQS, TOK))
        return jnp.where(lax.broadcasted_iota(jnp.int32, (SEQS, TOK), 0) == ids, 1.0, 0.0).astype(F32)

    def token_gates():
        need("seq", "gates", "cot")
        gates = gates_ref[...]
        hi = gates.astype(BF16).astype(F32)
        mid = (gates - hi).astype(BF16).astype(F32)
        low = (gates - hi - mid).astype(BF16).astype(F32)
        select = jnp.concatenate([onehot()] * 3, axis=0).T.astype(BF16)
        tg_v[...] = jnp.dot(
            select, jnp.concatenate([hi, mid, low], axis=0).astype(BF16), preferred_element_type=F32
        )
        for h in range(2):
            cols = slice(h * HALF, (h + 1) * HALF)
            sc[h] = (tg_v[:, cols] * cot_v[:, cols].astype(F32)).astype(BF16)
        send(sc, scs, tok_s.at[0], tok_r.at[0], sdev)

    def gelu(which):
        need("pre")
        xx = (xo, xh)[which]

        @pl.loop(0, NZ)
        def _(j):
            cols = pl.ds(pl.multiple_of((xx * NZ + j) * 128, 128), 128)
            u = pre_v[:, cols].astype(F32)
            sq = u * u
            th = jnp.tanh(0.7978845608 * (u + 0.044715 * sq * u))
            slope_v[:, cols] = 0.5 * (1.0 + th) + 0.5 * u * (1.0 - th * th) * 0.7978845608 * (
                1.0 + 3.0 * 0.044715 * sq
            )
            low_hidden = (0.5 * u * (1.0 + th)).astype(BF16)
            hid[:, cols] = low_hidden
            ht[xx, j] = low_hidden.T.reshape(2, ROWS, TOK)

        send(ht.at[xx, :, co], hts.at[xx], tok_s.at[1 + which], tok_r.at[1 + which], sdev)

    def once(key, *how):
        if key not in waited:
            waited.append(key)
            arrive(*how)

    def grad(h, rel):
        xx = (xh, xo)[rel]
        k = 2 - rel
        once("scs", scs, tok_s.at[0], tok_r.at[0], sdev)
        once(("hts", rel), hts.at[xx], tok_s.at[k], tok_r.at[k], sdev)
        mine = ht[xx, :, c].reshape(NZ * ROWS, TOK)
        other = hts[xx].reshape(NZ * ROWS, TOK)
        total = jnp.dot(mine, sc[h], preferred_element_type=F32)
        total += jnp.dot(other, scs[h], preferred_element_type=F32)
        part[h, xx] = (total * scaling).astype(BF16).reshape(NZ, ROWS, HALF)

    def sum_x(j):
        send(part.at[1, xo, zat(X_ORDER[j])], rx.at[j], rsx_s.at[j], rsx_r.at[j], xdev)

    sums = ((0, xo), (0, xh), (1, xh))

    def sum_z(stream, way, s):
        h, xx = sums[stream]
        off = (SUM_HOPS[stream][way] - s + 1) * (1 if way == 0 else -1)
        zz = zat(off)
        block = part.at[h, xx, zz]
        i = 8 * stream + 4 * way + s - 1
        if s > 1 or stream == 2:
            value = block[...].astype(F32)
            if stream == 2:
                jx = X_ORDER.index(4 if off == -4 else off)
                arrive(rx.at[jx], rsx_s.at[jx], rsx_r.at[jx], xdev)
                value += rx[jx].astype(F32)
            if s > 1:
                arrive(rz.at[i - 1], rsz_s.at[i - 1], rsz_r.at[i - 1], znext[way])
                value += rz[i - 1].astype(F32)
            block[...] = value.astype(BF16)
        send(block, rz.at[i], rsz_s.at[i], rsz_r.at[i], znext[way])

    def corrections():
        counter = jnp.full((1, HALF), step_ref[0, 0] + 1, jnp.int32)

        def power(base):
            total, factor = jnp.ones((1, HALF), F32), jnp.full((1, HALF), base, F32)
            for bit in range(7):
                on = jnp.bitwise_and(jnp.right_shift(counter, bit), 1) == 1
                total = jnp.where(on, total * factor, total)
                factor = factor * factor
            return total

        return 1.0 - power(0.9), 1.0 - power(0.999)

    def update(h, total):
        need("step", "m1", "m2")
        corr_first, corr_second = corrections()
        cols = slice(h * HALF, (h + 1) * HALF)
        first = 0.9 * m1_v[:, cols] + 0.1 * total
        second = 0.999 * m2_v[:, cols] + 0.001 * total * total
        fo_v[:, cols], so_v[:, cols] = first, second
        ratio = first / corr_first / (jnp.sqrt(second / corr_second) + 1e-08)
        master = w_v[:, cols]
        stepped = master - 0.01 * (ratio + 0.1 * master)
        st_s[h] = stepped.astype(BF16)
        send(st_s.at[h], st_r.at[h], go_s.at[h], go_r.at[h], up)
        st_v[h] = stepped

    def last(stream):
        h, xx = sums[stream]
        value = part[h, xx, z].astype(F32)
        if stream == 2:
            arrive(rx.at[7], rsx_s.at[7], rsx_r.at[7], xdev)
            value += rx[7].astype(F32)
        for way in range(2):
            i = 8 * stream + 4 * way + SUM_HOPS[stream][way] - 1
            arrive(rz.at[i], rsz_s.at[i], rsz_r.at[i], znext[way])
            value += rz[i].astype(F32)
        if stream == 0:
            part[0, xo, z] = value.astype(BF16)
            send(part.at[0, xo, z], rxa, rsx_s.at[8], rsx_r.at[8], xdev)
            return
        if stream == 1:
            arrive(rxa, rsx_s.at[8], rsx_r.at[8], xdev)
            value += rxa[...].astype(F32)
        update(h, value)

    def finish(h):
        cols = slice(h * HALF, (h + 1) * HALF)
        arrive(st_r.at[h], go_s.at[h], go_r.at[h], up)
        wo_v[:, cols] = 0.5 * (st_v[h] + st_r[h].astype(F32))

    def forward(h):
        for rel, xx, stream in ((0, xh, 2 * h), (1, xo, 1 + h)):
            for j in range(9):
                if j == 0 or (j - 1) % 4 < GATHER_HOPS[stream][(j - 1) // 4]:
                    i = 18 * h + 9 * rel + j
                    arrive(place(h, xx, zat(offset(j)), co), ags_s.at[i], ags_r.at[i], sdev)
        need("bi")
        cols = slice(h * HALF, (h + 1) * HALF)
        projected = jnp.dot(hid[...], wg[h].reshape(FFW, HALF), preferred_element_type=F32) * scaling
        bo_v[:, cols] = (bi_v[:, cols].astype(F32) + tg_v[:, cols] * projected).astype(BF16)
        product = cot_v[:, cols].astype(F32) * projected
        hi = product.astype(BF16)
        low = (product - hi.astype(F32)).astype(BF16)
        pick = onehot().astype(BF16)
        gl[h] = jnp.dot(pick, hi, preferred_element_type=F32) + jnp.dot(pick, low, preferred_element_type=F32)

    def gate(stage):
        if stage == 0:
            send(gl.at[co], gl_r, gg_ss.at[0], gg_rs.at[0], sdev)
        elif stage == 1:
            arrive(gl_r, gg_ss.at[0], gg_rs.at[0], sdev)
            chip = gl[c] + gl_r[...]
            gx[...] = jnp.concatenate([chip[:, :256], chip[:, 256:]], axis=0).astype(BF16)
            send(gx, gx_r, gg_ss.at[1], gg_rs.at[1], xdev)
        elif stage == 2:
            arrive(gx_r, gg_ss.at[1], gg_rs.at[1], xdev)
            gz[z] = (gx[...].astype(F32) + gx_r[...].astype(F32)).astype(BF16)
            for k in PEERS:
                send(gz.at[z], gz.at[z], gg_ss.at[1 + k], gg_rs.at[1 + k], dev(xh, zat(k), c))
        elif stage == 3:
            for k in PEERS:
                zz = zat(-k)
                arrive(gz.at[zz], gg_ss.at[1 + k], gg_rs.at[1 + k], dev(xh, zz, c))
            total = gz[0].astype(F32)
            for zz in range(1, NZ):
                total += gz[zz].astype(F32)
            gg_o[...] = jnp.concatenate([total[:SEQS], total[SEQS:]], axis=1)
            send(gg_o, gg_r, gg_ss.at[9], gg_rs.at[9], sdev)
            gg_v[:, pl.ds(pl.multiple_of(c * HALF, HALF), HALF)] = gg_o[...]
        else:
            arrive(gg_r, gg_ss.at[9], gg_rs.at[9], sdev)
            gg_v[:, pl.ds(pl.multiple_of(co * HALF, HALF), HALF)] = gg_r[...]

    def backward(q):
        cols = slice(q * HALF, (q + 1) * HALF)
        total = jnp.zeros((TOK, HALF), F32)
        for h in range(2):
            rows = wg[h, q * 8:(q + 1) * 8].reshape(HALF, HALF)
            total += lax.dot_general(sc[h], rows, (((1,), (1,)), ((), ())), preferred_element_type=F32)
        pg_v[:, cols] = (total * scaling * slope_v[:, cols]).astype(BF16)

    steps = dict(
        own=own, gz=pass_z, gx=pass_x, tg=token_gates, gelu=gelu, grad=grad, xs=sum_x, rs=sum_z,
        last=last, fin=finish, fwd=forward, gate=gate, bwd=backward,
    )
    for name, *detail in SCHEDULE:
        steps[name](*detail)
    for copy in sent:
        copy.wait_send()


def write_kernel(*refs):
    count = len(refs) // 2
    sources, targets, sems = refs[:count], refs[count:2 * count], refs[-1]
    copies = [pltpu.make_async_copy(a, b, sems.at[i]) for i, (a, b) in enumerate(zip(sources, targets))]
    for copy in copies:
        copy.start()
    for copy in copies:
        copy.wait()


def write_out(*arrays):
    return pl.pallas_call(
        write_kernel,
        out_shape=tuple(jax.ShapeDtypeStruct(a.shape, a.dtype) for a in arrays),
        in_specs=[pl.BlockSpec(memory_space=pl.ANY)] * len(arrays),
        out_specs=tuple(pl.BlockSpec(memory_space=pl.ANY) for _ in arrays),
        scratch_shapes=[pltpu.SemaphoreType.DMA((len(arrays),))],
        name="write_out",
    )(*arrays)


def fused(shift, place, *operands):
    vmem = pltpu.VMEM
    dma = pltpu.SemaphoreType.DMA
    return pl.pallas_call(
        functools.partial(kernel, shift),
        out_shape=(
            jax.ShapeDtypeStruct((TOK, D), BF16),
            jax.ShapeDtypeStruct((TOK, FFW), BF16),
            jax.ShapeDtypeStruct((SEQS, D), F32),
            jax.ShapeDtypeStruct((ROWS, D), F32),
            jax.ShapeDtypeStruct((ROWS, D), F32),
            jax.ShapeDtypeStruct((ROWS, D), F32),
        ),
        in_specs=[pl.BlockSpec(memory_space=pltpu.HBM)] * 9,
        out_specs=[pl.BlockSpec(memory_space=vmem)] * 6,
        scratch_shapes=[
            pltpu.SMEM((1, 1), jnp.int32), vmem((1, TOK), jnp.int32), vmem((SEQS, D), F32),
            vmem((ROWS, D), F32), vmem((ROWS, D), F32), vmem((ROWS, D), F32),
            vmem((TOK, FFW), BF16), vmem((TOK, D), BF16), vmem((TOK, D), BF16),
            vmem((2, 32, ROWS, HALF), BF16),
            vmem((TOK, FFW), BF16), vmem((TOK, FFW), F32),
            vmem((2, NZ, 2, ROWS, TOK), BF16), vmem((2, NZ, ROWS, TOK), BF16),
            vmem((2, TOK, HALF), BF16), vmem((2, TOK, HALF), BF16), vmem((TOK, D), F32),
            vmem((2, 2, NZ, ROWS, HALF), BF16), vmem((24, ROWS, HALF), BF16),
            vmem((NZ, ROWS, HALF), BF16), vmem((ROWS, HALF), BF16),
            vmem((2, SEQS, HALF), F32), vmem((SEQS, HALF), F32),
            vmem((2 * SEQS, HALF // 2), BF16), vmem((2 * SEQS, HALF // 2), BF16),
            vmem((NZ, 2 * SEQS, HALF // 2), BF16), vmem((SEQS, HALF), F32), vmem((SEQS, HALF), F32),
            vmem((2, ROWS, HALF), F32), vmem((2, ROWS, HALF), BF16), vmem((2, ROWS, HALF), BF16),
            dma((9,)),
            dma((24,)), dma((24,)), dma((18,)), dma((18,)), dma((36,)), dma((36,)),
            dma((3,)), dma((3,)), dma((24,)), dma((24,)), dma((9,)), dma((9,)),
            dma((10,)), dma((10,)), dma((2,)), dma((2,)),
        ],
        compiler_params=pltpu.CompilerParams(
            collective_id=place, has_side_effects=True, vmem_limit_bytes=48 << 20
        ),
        name="block_step",
    )(*operands)


def on_device(
    block_input, preact, cotangent, seq_ids, gates, weight, first_moment, second_moment, step
):
    operands = (
        step.reshape(1, 1), seq_ids, gates[0], weight[0], first_moment[0], second_moment[0],
        preact[0], cotangent[0], block_input[0],
    )
    levels = N_GOSSIP.bit_length() - 1
    branches = [functools.partial(fused, 1 << level, level) for level in range(levels)]
    results = lax.switch(lax.rem(step, levels), branches, *operands)
    return tuple(array[None] for array in write_out(*results))


def solution(mesh):
    split, whole = P("gossip", "fsdp", None), P("gossip", None, None)
    return jax.shard_map(
        on_device,
        mesh=mesh,
        in_specs=(split, split, split, P("gossip", "fsdp"), whole, split, split, split, P()),
        out_specs=(split, split, whole, split, split, split),
        check_vma=False,
    )
```

```python
import functools

import jax
import jax.numpy as jnp
from jax import lax
from jax.experimental import pallas as pl
from jax.experimental.pallas import tpu as pltpu
from jax.sharding import PartitionSpec as P

MESH = pl.DeviceIdType.MESH
BF16, F32 = jnp.bfloat16, jnp.float32

TOK, FFW, D, SEQS = 192, 2048, 1024, 8
ROWS, HALF = 64, 512
NZ = 8
N_GOSSIP = 16

GATHER_HOPS = ((4, 3), (3, 4), (4, 3))
SUM_HOPS = ((3, 4), (4, 3), (3, 4))
X_ORDER = (4, 3, -3, 2, -2, 1, -1, 0)
PEERS = tuple(range(1, NZ))
SCHEDULE = (
    ("own", 0, 0), ("own", 0, 2), ("own", 1, 1), ("own", 1, 2), ("gelu", 0), ("own", 1, 0), ("own", 0, 1), ("tg",),
    ("gz", 0, 0, 1), ("gz", 2, 1, 1), ("grad", 0, 1), ("grad", 1, 1), ("xs", 0), ("gz", 2, 0, 1), ("gx", 0, 0), ("rs", 0, 0, 1),
    ("rs", 0, 1, 1), ("gz", 2, 1, 2), ("gelu", 1), ("gz", 2, 0, 2), ("xs", 1), ("gz", 1, 1, 1), ("gz", 0, 1, 1), ("grad", 1, 0),
    ("xs", 2), ("gz", 0, 0, 2), ("xs", 3), ("gz", 1, 0, 1), ("grad", 0, 0), ("rs", 2, 1, 1), ("gx", 1, 2), ("gz", 2, 0, 3),
    ("rs", 1, 1, 1), ("rs", 1, 0, 1), ("gz", 1, 1, 2), ("gz", 0, 0, 3), ("rs", 0, 1, 2), ("xs", 4), ("gx", 1, 5), ("own", 1, 3),
    ("gz", 2, 1, 3), ("own", 0, 3), ("gz", 2, 0, 4), ("rs", 2, 1, 2), ("gx", 1, 0), ("gz", 0, 1, 2), ("xs", 5), ("rs", 2, 0, 1),
    ("gz", 1, 0, 2), ("xs", 6), ("xs", 7), ("gx", 1, 1), ("gx", 1, 3), ("gz", 1, 1, 3), ("rs", 0, 0, 2), ("rs", 0, 1, 3),
    ("rs", 2, 1, 3), ("gx", 1, 6), ("rs", 1, 0, 2), ("gz", 0, 1, 3), ("gx", 1, 4), ("gx", 1, 7), ("rs", 1, 1, 2),
    ("rs", 2, 0, 2), ("gz", 0, 0, 4), ("rs", 0, 0, 3), ("gz", 1, 1, 4), ("gz", 1, 0, 3), ("fwd", 1), ("rs", 1, 0, 3),
    ("rs", 0, 1, 4), ("fwd", 0), ("rs", 2, 1, 4), ("gate", 0), ("rs", 2, 0, 3), ("gate", 1), ("bwd", 3), ("rs", 1, 0, 4),
    ("rs", 1, 1, 3), ("last", 0), ("last", 2), ("gate", 2), ("bwd", 1), ("bwd", 0), ("bwd", 2), ("last", 1), ("fin", 1),
    ("gate", 3), ("gate", 4), ("fin", 0),
)


def kernel(
    shift,
    step_h, seq_h, gates_h, w_h, m1_h, m2_h, pre_h, cot_h, bi_h,
    bo_v, pg_v, gg_v, wo_v, fo_v, so_v,
    step_ref, seq_ref, gates_ref, w_v, m1_v, m2_v, pre_v, cot_v, bi_v,
    wg, hid, slope_v, ht, hts, sc, scs, tg_v,
    part, rz, rx, rxa,
    gl, gl_r, gx, gx_r, gz, gg_o, gg_r,
    st_v, st_s, st_r,
    lsem,
    agz_s, agz_r, agx_s, agx_r, ags_s, ags_r,
    tok_s, tok_r, rsz_s, rsz_r, rsx_s, rsx_r, gg_ss, gg_rs, go_s, go_r,
):
    g = lax.axis_index("gossip")
    f = lax.axis_index("fsdp")
    xh = lax.div(f, 16)
    z = lax.rem(lax.div(f, 2), NZ)
    c = lax.rem(f, 2)
    xo, co = 1 - xh, 1 - c
    scaling = FFW ** -0.5

    def zat(k):
        return lax.rem(z + (k % NZ), NZ)

    def dev(xx, zz, cc):
        return {"fsdp": xx * 16 + zz * 2 + cc}

    znext = (dev(xh, zat(1), c), dev(xh, zat(-1), c))
    xdev, sdev = dev(xo, z, c), dev(xh, z, co)
    up = {"gossip": lax.rem(g + shift, N_GOSSIP)}
    down = {"gossip": lax.rem(g + N_GOSSIP - shift, N_GOSSIP)}

    sent = []

    def describe(src, dst, ssem, rsem, to):
        return pltpu.make_async_remote_copy(
            src_ref=src, dst_ref=dst, send_sem=ssem, recv_sem=rsem, device_id=to, device_id_type=MESH
        )

    def send(src, dst, ssem, rsem, to):
        copy = describe(src, dst, ssem, rsem, to)
        copy.start()
        sent.append(copy)

    def arrive(dst, ssem, rsem, to):
        describe(dst, dst, ssem, rsem, to).wait_recv()

    loads = {}

    def load(name, src, dst):
        loads[name] = pltpu.make_async_copy(src, dst, lsem.at[len(loads)])
        loads[name].start()

    def need(*wanted):
        for name in wanted:
            if name in loads:
                loads.pop(name).wait()
                waited.append(name)

    waited = []
    load("w", w_h, w_v)
    barrier = pltpu.get_barrier_semaphore()
    greeted = [xdev, sdev, down] + [dev(xh, zat(k), c) for k in PEERS]
    for to in greeted:
        pl.semaphore_signal(barrier, inc=1, device_id=to, device_id_type=MESH)
    rest = (
        ("seq", seq_h, seq_ref), ("gates", gates_h, gates_ref), ("cot", cot_h, cot_v), ("pre", pre_h, pre_v),
        ("bi", bi_h, bi_v), ("step", step_h, step_ref), ("m1", m1_h, m1_v), ("m2", m2_h, m2_v),
    )
    for item in rest:
        load(*item)

    def place(h, xx, zz, cc):
        return wg.at[h, xx * 16 + zz * 2 + cc]

    need("w")
    for h in range(2):
        wg[h, f] = w_v[:, h * HALF:(h + 1) * HALF].astype(BF16)
    pl.semaphore_wait(barrier, len(greeted))

    def send_x(h, j, zz):
        block = place(h, xh, zz, c)
        i = 9 * h + j
        send(block, block, agx_s.at[i], agx_r.at[i], xdev)

    def send_s(h, rel, j, xx, zz):
        block = place(h, xx, zz, c)
        i = 18 * h + 9 * rel + j
        send(block, block, ags_s.at[i], ags_r.at[i], sdev)

    def send_z(stream, way, s, h, xx, zz):
        block = place(h, xx, zz, c)
        i = 8 * stream + 4 * way + s - 1
        send(block, block, agz_s.at[i], agz_r.at[i], znext[way])

    def own(h, link):
        if link < 2:
            send_z(2 * h, link, 1, h, xh, z)
        elif link == 2:
            send_x(h, 0, z)
        else:
            send_s(h, 0, 0, xh, z)

    def pass_z(stream, way, s):
        h, xx, rel = ((0, xh, 0), (0, xo, 1), (1, xh, 0))[stream]
        zz = zat(-s if way == 0 else s)
        i = 8 * stream + 4 * way + s - 1
        arrive(place(h, xx, zz, c), agz_s.at[i], agz_r.at[i], znext[way])
        if s < GATHER_HOPS[stream][way]:
            send_z(stream, way, s + 1, h, xx, zz)
        j = 4 * way + s
        if stream == 2:
            send_x(1, j, zz)
        send_s(h, rel, j, xx, zz)

    def offset(j):
        return 0 if j == 0 else -j if j <= 4 else j - 4

    def pass_x(h, j):
        zz = zat(offset(j))
        i = 9 * h + j
        arrive(place(h, xo, zz, c), agx_s.at[i], agx_r.at[i], xdev)
        if h == 0:
            for way in range(2):
                send_z(1, way, 1, 0, xo, zz)
        send_s(h, 1, j, xo, zz)

    def onehot():
        ids = jnp.broadcast_to(seq_ref[...], (SEQS, TOK))
        return jnp.where(lax.broadcasted_iota(jnp.int32, (SEQS, TOK), 0) == ids, 1.0, 0.0).astype(F32)

    def token_gates():
        need("seq", "gates", "cot")
        gates = gates_ref[...]
        hi = gates.astype(BF16).astype(F32)
        mid = (gates - hi).astype(BF16).astype(F32)
        low = (gates - hi - mid).astype(BF16).astype(F32)
        select = jnp.concatenate([onehot()] * 3, axis=0).T.astype(BF16)
        tg_v[...] = jnp.dot(
            select, jnp.concatenate([hi, mid, low], axis=0).astype(BF16), preferred_element_type=F32
        )
        for h in range(2):
            cols = slice(h * HALF, (h + 1) * HALF)
            sc[h] = (tg_v[:, cols] * cot_v[:, cols].astype(F32)).astype(BF16)
        send(sc, scs, tok_s.at[0], tok_r.at[0], sdev)

    def gelu(which):
        need("pre")
        xx = (xo, xh)[which]

        @pl.loop(0, NZ)
        def _(j):
            cols = pl.ds(pl.multiple_of((xx * NZ + j) * 128, 128), 128)
            u = pre_v[:, cols].astype(F32)
            sq = u * u
            th = jnp.tanh(0.7978845608 * (u + 0.044715 * sq * u))
            slope_v[:, cols] = 0.5 * (1.0 + th) + 0.5 * u * (1.0 - th * th) * 0.7978845608 * (
                1.0 + 3.0 * 0.044715 * sq
            )
            low_hidden = (0.5 * u * (1.0 + th)).astype(BF16)
            hid[:, cols] = low_hidden
            ht[xx, j] = low_hidden.T.reshape(2, ROWS, TOK)

        send(ht.at[xx, :, co], hts.at[xx], tok_s.at[1 + which], tok_r.at[1 + which], sdev)

    def once(key, *how):
        if key not in waited:
            waited.append(key)
            arrive(*how)

    def grad(h, rel):
        xx = (xh, xo)[rel]
        k = 2 - rel
        once("scs", scs, tok_s.at[0], tok_r.at[0], sdev)
        once(("hts", rel), hts.at[xx], tok_s.at[k], tok_r.at[k], sdev)
        mine = ht[xx, :, c].reshape(NZ * ROWS, TOK)
        other = hts[xx].reshape(NZ * ROWS, TOK)
        total = jnp.dot(mine, sc[h], preferred_element_type=F32)
        total += jnp.dot(other, scs[h], preferred_element_type=F32)
        part[h, xx] = (total * scaling).astype(BF16).reshape(NZ, ROWS, HALF)

    def sum_x(j):
        send(part.at[1, xo, zat(X_ORDER[j])], rx.at[j], rsx_s.at[j], rsx_r.at[j], xdev)

    sums = ((0, xo), (0, xh), (1, xh))

    def sum_z(stream, way, s):
        h, xx = sums[stream]
        off = (SUM_HOPS[stream][way] - s + 1) * (1 if way == 0 else -1)
        zz = zat(off)
        block = part.at[h, xx, zz]
        i = 8 * stream + 4 * way + s - 1
        if s > 1 or stream == 2:
            value = block[...].astype(F32)
            if stream == 2:
                jx = X_ORDER.index(4 if off == -4 else off)
                arrive(rx.at[jx], rsx_s.at[jx], rsx_r.at[jx], xdev)
                value += rx[jx].astype(F32)
            if s > 1:
                arrive(rz.at[i - 1], rsz_s.at[i - 1], rsz_r.at[i - 1], znext[way])
                value += rz[i - 1].astype(F32)
            block[...] = value.astype(BF16)
        send(block, rz.at[i], rsz_s.at[i], rsz_r.at[i], znext[way])

    def corrections():
        counter = jnp.full((1, HALF), step_ref[0, 0] + 1, jnp.int32)

        def power(base):
            total, factor = jnp.ones((1, HALF), F32), jnp.full((1, HALF), base, F32)
            for bit in range(7):
                on = jnp.bitwise_and(jnp.right_shift(counter, bit), 1) == 1
                total = jnp.where(on, total * factor, total)
                factor = factor * factor
            return total

        return 1.0 - power(0.9), 1.0 - power(0.999)

    def update(h, total):
        need("step", "m1", "m2")
        corr_first, corr_second = corrections()
        cols = slice(h * HALF, (h + 1) * HALF)
        first = 0.9 * m1_v[:, cols] + 0.1 * total
        second = 0.999 * m2_v[:, cols] + 0.001 * total * total
        fo_v[:, cols], so_v[:, cols] = first, second
        ratio = first / corr_first / (jnp.sqrt(second / corr_second) + 1e-08)
        master = w_v[:, cols]
        stepped = master - 0.01 * (ratio + 0.1 * master)
        st_s[h] = stepped.astype(BF16)
        send(st_s.at[h], st_r.at[h], go_s.at[h], go_r.at[h], up)
        st_v[h] = stepped

    def last(stream):
        h, xx = sums[stream]
        value = part[h, xx, z].astype(F32)
        if stream == 2:
            arrive(rx.at[7], rsx_s.at[7], rsx_r.at[7], xdev)
            value += rx[7].astype(F32)
        for way in range(2):
            i = 8 * stream + 4 * way + SUM_HOPS[stream][way] - 1
            arrive(rz.at[i], rsz_s.at[i], rsz_r.at[i], znext[way])
            value += rz[i].astype(F32)
        if stream == 0:
            part[0, xo, z] = value.astype(BF16)
            send(part.at[0, xo, z], rxa, rsx_s.at[8], rsx_r.at[8], xdev)
            return
        if stream == 1:
            arrive(rxa, rsx_s.at[8], rsx_r.at[8], xdev)
            value += rxa[...].astype(F32)
        update(h, value)

    def finish(h):
        cols = slice(h * HALF, (h + 1) * HALF)
        arrive(st_r.at[h], go_s.at[h], go_r.at[h], up)
        wo_v[:, cols] = 0.5 * (st_v[h] + st_r[h].astype(F32))

    def forward(h):
        for rel, xx, stream in ((0, xh, 2 * h), (1, xo, 1 + h)):
            for j in range(9):
                if j == 0 or (j - 1) % 4 < GATHER_HOPS[stream][(j - 1) // 4]:
                    i = 18 * h + 9 * rel + j
                    arrive(place(h, xx, zat(offset(j)), co), ags_s.at[i], ags_r.at[i], sdev)
        need("bi")
        cols = slice(h * HALF, (h + 1) * HALF)
        projected = jnp.dot(hid[...], wg[h].reshape(FFW, HALF), preferred_element_type=F32) * scaling
        bo_v[:, cols] = (bi_v[:, cols].astype(F32) + tg_v[:, cols] * projected).astype(BF16)
        product = cot_v[:, cols].astype(F32) * projected
        hi = product.astype(BF16)
        low = (product - hi.astype(F32)).astype(BF16)
        pick = onehot().astype(BF16)
        gl[h] = jnp.dot(pick, hi, preferred_element_type=F32) + jnp.dot(pick, low, preferred_element_type=F32)

    def gate(stage):
        if stage == 0:
            send(gl.at[co], gl_r, gg_ss.at[0], gg_rs.at[0], sdev)
        elif stage == 1:
            arrive(gl_r, gg_ss.at[0], gg_rs.at[0], sdev)
            chip = gl[c] + gl_r[...]
            gx[...] = jnp.concatenate([chip[:, :256], chip[:, 256:]], axis=0).astype(BF16)
            send(gx, gx_r, gg_ss.at[1], gg_rs.at[1], xdev)
        elif stage == 2:
            arrive(gx_r, gg_ss.at[1], gg_rs.at[1], xdev)
            gz[z] = (gx[...].astype(F32) + gx_r[...].astype(F32)).astype(BF16)
            for k in PEERS:
                send(gz.at[z], gz.at[z], gg_ss.at[1 + k], gg_rs.at[1 + k], dev(xh, zat(k), c))
        elif stage == 3:
            for k in PEERS:
                zz = zat(-k)
                arrive(gz.at[zz], gg_ss.at[1 + k], gg_rs.at[1 + k], dev(xh, zz, c))
            total = gz[0].astype(F32)
            for zz in range(1, NZ):
                total += gz[zz].astype(F32)
            gg_o[...] = jnp.concatenate([total[:SEQS], total[SEQS:]], axis=1)
            send(gg_o, gg_r, gg_ss.at[9], gg_rs.at[9], sdev)
            gg_v[:, pl.ds(pl.multiple_of(c * HALF, HALF), HALF)] = gg_o[...]
        else:
            arrive(gg_r, gg_ss.at[9], gg_rs.at[9], sdev)
            gg_v[:, pl.ds(pl.multiple_of(co * HALF, HALF), HALF)] = gg_r[...]

    def backward(q):
        cols = slice(q * HALF, (q + 1) * HALF)
        total = jnp.zeros((TOK, HALF), F32)
        for h in range(2):
            rows = wg[h, q * 8:(q + 1) * 8].reshape(HALF, HALF)
            total += lax.dot_general(sc[h], rows, (((1,), (1,)), ((), ())), preferred_element_type=F32)
        pg_v[:, cols] = (total * scaling * slope_v[:, cols]).astype(BF16)

    steps = dict(
        own=own, gz=pass_z, gx=pass_x, tg=token_gates, gelu=gelu, grad=grad, xs=sum_x, rs=sum_z,
        last=last, fin=finish, fwd=forward, gate=gate, bwd=backward,
    )
    for name, *detail in SCHEDULE:
        steps[name](*detail)
    for copy in sent:
        copy.wait_send()


def write_kernel(*refs):
    count = len(refs) // 2
    sources, targets, sems = refs[:count], refs[count:2 * count], refs[-1]
    copies = [pltpu.make_async_copy(a, b, sems.at[i]) for i, (a, b) in enumerate(zip(sources, targets))]
    for copy in copies:
        copy.start()
    for copy in copies:
        copy.wait()


def write_out(*arrays):
    return pl.pallas_call(
        write_kernel,
        out_shape=tuple(jax.ShapeDtypeStruct(a.shape, a.dtype) for a in arrays),
        in_specs=[pl.BlockSpec(memory_space=pl.ANY)] * len(arrays),
        out_specs=tuple(pl.BlockSpec(memory_space=pl.ANY) for _ in arrays),
        scratch_shapes=[pltpu.SemaphoreType.DMA((len(arrays),))],
        name="write_out",
    )(*arrays)


def fused(shift, place, *operands):
    vmem = pltpu.VMEM
    dma = pltpu.SemaphoreType.DMA
    return pl.pallas_call(
        functools.partial(kernel, shift),
        out_shape=(
            jax.ShapeDtypeStruct((TOK, D), BF16),
            jax.ShapeDtypeStruct((TOK, FFW), BF16),
            jax.ShapeDtypeStruct((SEQS, D), F32),
            jax.ShapeDtypeStruct((ROWS, D), F32),
            jax.ShapeDtypeStruct((ROWS, D), F32),
            jax.ShapeDtypeStruct((ROWS, D), F32),
        ),
        in_specs=[pl.BlockSpec(memory_space=pltpu.HBM)] * 9,
        out_specs=[pl.BlockSpec(memory_space=vmem)] * 6,
        scratch_shapes=[
            pltpu.SMEM((1, 1), jnp.int32), vmem((1, TOK), jnp.int32), vmem((SEQS, D), F32),
            vmem((ROWS, D), F32), vmem((ROWS, D), F32), vmem((ROWS, D), F32),
            vmem((TOK, FFW), BF16), vmem((TOK, D), BF16), vmem((TOK, D), BF16),
            vmem((2, 32, ROWS, HALF), BF16),
            vmem((TOK, FFW), BF16), vmem((TOK, FFW), F32),
            vmem((2, NZ, 2, ROWS, TOK), BF16), vmem((2, NZ, ROWS, TOK), BF16),
            vmem((2, TOK, HALF), BF16), vmem((2, TOK, HALF), BF16), vmem((TOK, D), F32),
            vmem((2, 2, NZ, ROWS, HALF), BF16), vmem((24, ROWS, HALF), BF16),
            vmem((NZ, ROWS, HALF), BF16), vmem((ROWS, HALF), BF16),
            vmem((2, SEQS, HALF), F32), vmem((SEQS, HALF), F32),
            vmem((2 * SEQS, HALF // 2), BF16), vmem((2 * SEQS, HALF // 2), BF16),
            vmem((NZ, 2 * SEQS, HALF // 2), BF16), vmem((SEQS, HALF), F32), vmem((SEQS, HALF), F32),
            vmem((2, ROWS, HALF), F32), vmem((2, ROWS, HALF), BF16), vmem((2, ROWS, HALF), BF16),
            dma((9,)),
            dma((24,)), dma((24,)), dma((18,)), dma((18,)), dma((36,)), dma((36,)),
            dma((3,)), dma((3,)), dma((24,)), dma((24,)), dma((9,)), dma((9,)),
            dma((10,)), dma((10,)), dma((2,)), dma((2,)),
        ],
        compiler_params=pltpu.CompilerParams(
            collective_id=place, has_side_effects=True, vmem_limit_bytes=48 << 20
        ),
        name="block_step",
    )(*operands)


def on_device(
    block_input, preact, cotangent, seq_ids, gates, weight, first_moment, second_moment, step
):
    operands = (
        step.reshape(1, 1), seq_ids, gates[0], weight[0], first_moment[0], second_moment[0],
        preact[0], cotangent[0], block_input[0],
    )
    levels = N_GOSSIP.bit_length() - 1
    branches = [functools.partial(fused, 1 << level, level) for level in range(levels)]
    results = lax.switch(lax.rem(step, levels), branches, *operands)
    return tuple(array[None] for array in write_out(*results))


def solution(mesh):
    split, whole = P("gossip", "fsdp", None), P("gossip", None, None)
    return jax.shard_map(
        on_device,
        mesh=mesh,
        in_specs=(split, split, split, P("gossip", "fsdp"), whole, split, split, split, P()),
        out_specs=(split, split, whole, split, split, split),
        check_vma=False,
    )
```

```python
import functools

import jax
import jax.numpy as jnp
from jax import lax
from jax.experimental import pallas as pl
from jax.experimental.pallas import tpu as pltpu
from jax.sharding import PartitionSpec as P

MESH = pl.DeviceIdType.MESH
BF16, F32 = jnp.bfloat16, jnp.float32

TOK, FFW, D, SEQS = 192, 2048, 1024, 8
ROWS, HALF = 64, 512
NZ = 8
N_GOSSIP = 16

GATHER_HOPS = ((4, 3), (3, 4), (4, 3))
SUM_HOPS = ((3, 4), (4, 3), (3, 4))
X_ORDER = (4, 3, -3, 2, -2, 1, -1, 0)
PEERS = tuple(range(1, NZ))
SCHEDULE = (
    ("own", 0, 0), ("own", 0, 2), ("own", 1, 1), ("own", 1, 2), ("gelu", 0), ("own", 1, 0), ("own", 0, 1), ("tg",),
    ("gz", 0, 0, 1), ("gz", 2, 1, 1), ("grad", 0, 1), ("grad", 1, 1), ("xs", 0), ("gz", 2, 0, 1), ("gx", 0, 0), ("rs", 0, 0, 1),
    ("rs", 0, 1, 1), ("gz", 2, 1, 2), ("gelu", 1), ("gz", 2, 0, 2), ("xs", 1), ("gz", 1, 1, 1), ("gz", 0, 1, 1), ("grad", 1, 0),
    ("xs", 2), ("gz", 0, 0, 2), ("xs", 3), ("gz", 1, 0, 1), ("grad", 0, 0), ("rs", 2, 1, 1), ("gx", 1, 2), ("gz", 2, 0, 3),
    ("rs", 1, 1, 1), ("rs", 1, 0, 1), ("gz", 1, 1, 2), ("gz", 0, 0, 3), ("rs", 0, 1, 2), ("xs", 4), ("gx", 1, 5), ("own", 1, 3),
    ("gz", 2, 1, 3), ("own", 0, 3), ("gz", 2, 0, 4), ("rs", 2, 1, 2), ("gx", 1, 0), ("gz", 0, 1, 2), ("xs", 5), ("rs", 2, 0, 1),
    ("gz", 1, 0, 2), ("xs", 6), ("xs", 7), ("gx", 1, 1), ("gx", 1, 3), ("gz", 1, 1, 3), ("rs", 0, 0, 2), ("rs", 0, 1, 3),
    ("rs", 2, 1, 3), ("gx", 1, 6), ("rs", 1, 0, 2), ("gz", 0, 1, 3), ("gx", 1, 4), ("gx", 1, 7), ("rs", 1, 1, 2),
    ("rs", 2, 0, 2), ("gz", 0, 0, 4), ("rs", 0, 0, 3), ("gz", 1, 1, 4), ("gz", 1, 0, 3), ("fwd", 1), ("rs", 1, 0, 3),
    ("rs", 0, 1, 4), ("fwd", 0), ("rs", 2, 1, 4), ("gate", 0), ("rs", 2, 0, 3), ("gate", 1), ("bwd", 3), ("rs", 1, 0, 4),
    ("rs", 1, 1, 3), ("last", 0), ("last", 2), ("gate", 2), ("bwd", 1), ("bwd", 0), ("bwd", 2), ("last", 1), ("fin", 1),
    ("gate", 3), ("gate", 4), ("fin", 0),
)


def kernel(
    shift,
    step_h, seq_h, gates_h, w_h, m1_h, m2_h, pre_h, cot_h, bi_h,
    bo_v, pg_v, gg_v, wo_v, fo_v, so_v,
    step_ref, seq_ref, gates_ref, w_v, m1_v, m2_v, pre_v, cot_v, bi_v,
    wg, hid, slope_v, ht, hts, sc, scs, tg_v,
    part, rz, rx, rxa,
    gl, gl_r, gx, gx_r, gz, gg_o, gg_r,
    st_v, st_s, st_r,
    lsem,
    agz_s, agz_r, agx_s, agx_r, ags_s, ags_r,
    tok_s, tok_r, rsz_s, rsz_r, rsx_s, rsx_r, gg_ss, gg_rs, go_s, go_r,
):
    g = lax.axis_index("gossip")
    f = lax.axis_index("fsdp")
    xh = lax.div(f, 16)
    z = lax.rem(lax.div(f, 2), NZ)
    c = lax.rem(f, 2)
    xo, co = 1 - xh, 1 - c
    scaling = FFW ** -0.5

    def zat(k):
        return lax.rem(z + (k % NZ), NZ)

    def dev(xx, zz, cc):
        return {"fsdp": xx * 16 + zz * 2 + cc}

    znext = (dev(xh, zat(1), c), dev(xh, zat(-1), c))
    xdev, sdev = dev(xo, z, c), dev(xh, z, co)
    up = {"gossip": lax.rem(g + shift, N_GOSSIP)}
    down = {"gossip": lax.rem(g + N_GOSSIP - shift, N_GOSSIP)}

    sent = []

    def describe(src, dst, ssem, rsem, to):
        return pltpu.make_async_remote_copy(
            src_ref=src, dst_ref=dst, send_sem=ssem, recv_sem=rsem, device_id=to, device_id_type=MESH
        )

    def send(src, dst, ssem, rsem, to):
        copy = describe(src, dst, ssem, rsem, to)
        copy.start()
        sent.append(copy)

    def arrive(dst, ssem, rsem, to):
        describe(dst, dst, ssem, rsem, to).wait_recv()

    loads = {}

    def load(name, src, dst):
        loads[name] = pltpu.make_async_copy(src, dst, lsem.at[len(loads)])
        loads[name].start()

    def need(*wanted):
        for name in wanted:
            if name in loads:
                loads.pop(name).wait()
                waited.append(name)

    waited = []
    load("w", w_h, w_v)
    barrier = pltpu.get_barrier_semaphore()
    greeted = [xdev, sdev, down] + [dev(xh, zat(k), c) for k in PEERS]
    for to in greeted:
        pl.semaphore_signal(barrier, inc=1, device_id=to, device_id_type=MESH)
    rest = (
        ("seq", seq_h, seq_ref), ("gates", gates_h, gates_ref), ("cot", cot_h, cot_v), ("pre", pre_h, pre_v),
        ("bi", bi_h, bi_v), ("step", step_h, step_ref), ("m1", m1_h, m1_v), ("m2", m2_h, m2_v),
    )
    for item in rest:
        load(*item)

    def place(h, xx, zz, cc):
        return wg.at[h, xx * 16 + zz * 2 + cc]

    need("w")
    for h in range(2):
        wg[h, f] = w_v[:, h * HALF:(h + 1) * HALF].astype(BF16)
    pl.semaphore_wait(barrier, len(greeted))

    def send_x(h, j, zz):
        block = place(h, xh, zz, c)
        i = 9 * h + j
        send(block, block, agx_s.at[i], agx_r.at[i], xdev)

    def send_s(h, rel, j, xx, zz):
        block = place(h, xx, zz, c)
        i = 18 * h + 9 * rel + j
        send(block, block, ags_s.at[i], ags_r.at[i], sdev)

    def send_z(stream, way, s, h, xx, zz):
        block = place(h, xx, zz, c)
        i = 8 * stream + 4 * way + s - 1
        send(block, block, agz_s.at[i], agz_r.at[i], znext[way])

    def own(h, link):
        if link < 2:
            send_z(2 * h, link, 1, h, xh, z)
        elif link == 2:
            send_x(h, 0, z)
        else:
            send_s(h, 0, 0, xh, z)

    def pass_z(stream, way, s):
        h, xx, rel = ((0, xh, 0), (0, xo, 1), (1, xh, 0))[stream]
        zz = zat(-s if way == 0 else s)
        i = 8 * stream + 4 * way + s - 1
        arrive(place(h, xx, zz, c), agz_s.at[i], agz_r.at[i], znext[way])
        if s < GATHER_HOPS[stream][way]:
            send_z(stream, way, s + 1, h, xx, zz)
        j = 4 * way + s
        if stream == 2:
            send_x(1, j, zz)
        send_s(h, rel, j, xx, zz)

    def offset(j):
        return 0 if j == 0 else -j if j <= 4 else j - 4

    def pass_x(h, j):
        zz = zat(offset(j))
        i = 9 * h + j
        arrive(place(h, xo, zz, c), agx_s.at[i], agx_r.at[i], xdev)
        if h == 0:
            for way in range(2):
                send_z(1, way, 1, 0, xo, zz)
        send_s(h, 1, j, xo, zz)

    def onehot():
        ids = jnp.broadcast_to(seq_ref[...], (SEQS, TOK))
        return jnp.where(lax.broadcasted_iota(jnp.int32, (SEQS, TOK), 0) == ids, 1.0, 0.0).astype(F32)

    def token_gates():
        need("seq", "gates", "cot")
        gates = gates_ref[...]
        hi = gates.astype(BF16).astype(F32)
        mid = (gates - hi).astype(BF16).astype(F32)
        low = (gates - hi - mid).astype(BF16).astype(F32)
        select = jnp.concatenate([onehot()] * 3, axis=0).T.astype(BF16)
        tg_v[...] = jnp.dot(
            select, jnp.concatenate([hi, mid, low], axis=0).astype(BF16), preferred_element_type=F32
        )
        for h in range(2):
            cols = slice(h * HALF, (h + 1) * HALF)
            sc[h] = (tg_v[:, cols] * cot_v[:, cols].astype(F32)).astype(BF16)
        send(sc, scs, tok_s.at[0], tok_r.at[0], sdev)

    def gelu(which):
        need("pre")
        xx = (xo, xh)[which]

        @pl.loop(0, NZ)
        def _(j):
            cols = pl.ds(pl.multiple_of((xx * NZ + j) * 128, 128), 128)
            u = pre_v[:, cols].astype(F32)
            sq = u * u
            th = jnp.tanh(0.7978845608 * (u + 0.044715 * sq * u))
            slope_v[:, cols] = 0.5 * (1.0 + th) + 0.5 * u * (1.0 - th * th) * 0.7978845608 * (
                1.0 + 3.0 * 0.044715 * sq
            )
            low_hidden = (0.5 * u * (1.0 + th)).astype(BF16)
            hid[:, cols] = low_hidden
            ht[xx, j] = low_hidden.T.reshape(2, ROWS, TOK)

        send(ht.at[xx, :, co], hts.at[xx], tok_s.at[1 + which], tok_r.at[1 + which], sdev)

    def once(key, *how):
        if key not in waited:
            waited.append(key)
            arrive(*how)

    def grad(h, rel):
        xx = (xh, xo)[rel]
        k = 2 - rel
        once("scs", scs, tok_s.at[0], tok_r.at[0], sdev)
        once(("hts", rel), hts.at[xx], tok_s.at[k], tok_r.at[k], sdev)
        mine = ht[xx, :, c].reshape(NZ * ROWS, TOK)
        other = hts[xx].reshape(NZ * ROWS, TOK)
        total = jnp.dot(mine, sc[h], preferred_element_type=F32)
        total += jnp.dot(other, scs[h], preferred_element_type=F32)
        part[h, xx] = (total * scaling).astype(BF16).reshape(NZ, ROWS, HALF)

    def sum_x(j):
        send(part.at[1, xo, zat(X_ORDER[j])], rx.at[j], rsx_s.at[j], rsx_r.at[j], xdev)

    sums = ((0, xo), (0, xh), (1, xh))

    def sum_z(stream, way, s):
        h, xx = sums[stream]
        off = (SUM_HOPS[stream][way] - s + 1) * (1 if way == 0 else -1)
        zz = zat(off)
        block = part.at[h, xx, zz]
        i = 8 * stream + 4 * way + s - 1
        if s > 1 or stream == 2:
            value = block[...].astype(F32)
            if stream == 2:
                jx = X_ORDER.index(4 if off == -4 else off)
                arrive(rx.at[jx], rsx_s.at[jx], rsx_r.at[jx], xdev)
                value += rx[jx].astype(F32)
            if s > 1:
                arrive(rz.at[i - 1], rsz_s.at[i - 1], rsz_r.at[i - 1], znext[way])
                value += rz[i - 1].astype(F32)
            block[...] = value.astype(BF16)
        send(block, rz.at[i], rsz_s.at[i], rsz_r.at[i], znext[way])

    def corrections():
        counter = jnp.full((1, HALF), step_ref[0, 0] + 1, jnp.int32)

        def power(base):
            total, factor = jnp.ones((1, HALF), F32), jnp.full((1, HALF), base, F32)
            for bit in range(7):
                on = jnp.bitwise_and(jnp.right_shift(counter, bit), 1) == 1
                total = jnp.where(on, total * factor, total)
                factor = factor * factor
            return total

        return 1.0 - power(0.9), 1.0 - power(0.999)

    def update(h, total):
        need("step", "m1", "m2")
        corr_first, corr_second = corrections()
        cols = slice(h * HALF, (h + 1) * HALF)
        first = 0.9 * m1_v[:, cols] + 0.1 * total
        second = 0.999 * m2_v[:, cols] + 0.001 * total * total
        fo_v[:, cols], so_v[:, cols] = first, second
        ratio = first / corr_first / (jnp.sqrt(second / corr_second) + 1e-08)
        master = w_v[:, cols]
        stepped = master - 0.01 * (ratio + 0.1 * master)
        st_s[h] = stepped.astype(BF16)
        send(st_s.at[h], st_r.at[h], go_s.at[h], go_r.at[h], up)
        st_v[h] = stepped

    def last(stream):
        h, xx = sums[stream]
        value = part[h, xx, z].astype(F32)
        if stream == 2:
            arrive(rx.at[7], rsx_s.at[7], rsx_r.at[7], xdev)
            value += rx[7].astype(F32)
        for way in range(2):
            i = 8 * stream + 4 * way + SUM_HOPS[stream][way] - 1
            arrive(rz.at[i], rsz_s.at[i], rsz_r.at[i], znext[way])
            value += rz[i].astype(F32)
        if stream == 0:
            part[0, xo, z] = value.astype(BF16)
            send(part.at[0, xo, z], rxa, rsx_s.at[8], rsx_r.at[8], xdev)
            return
        if stream == 1:
            arrive(rxa, rsx_s.at[8], rsx_r.at[8], xdev)
            value += rxa[...].astype(F32)
        update(h, value)

    def finish(h):
        cols = slice(h * HALF, (h + 1) * HALF)
        arrive(st_r.at[h], go_s.at[h], go_r.at[h], up)
        wo_v[:, cols] = 0.5 * (st_v[h] + st_r[h].astype(F32))

    def forward(h):
        for rel, xx, stream in ((0, xh, 2 * h), (1, xo, 1 + h)):
            for j in range(9):
                if j == 0 or (j - 1) % 4 < GATHER_HOPS[stream][(j - 1) // 4]:
                    i = 18 * h + 9 * rel + j
                    arrive(place(h, xx, zat(offset(j)), co), ags_s.at[i], ags_r.at[i], sdev)
        need("bi")
        cols = slice(h * HALF, (h + 1) * HALF)
        projected = jnp.dot(hid[...], wg[h].reshape(FFW, HALF), preferred_element_type=F32) * scaling
        bo_v[:, cols] = (bi_v[:, cols].astype(F32) + tg_v[:, cols] * projected).astype(BF16)
        product = cot_v[:, cols].astype(F32) * projected
        hi = product.astype(BF16)
        low = (product - hi.astype(F32)).astype(BF16)
        pick = onehot().astype(BF16)
        gl[h] = jnp.dot(pick, hi, preferred_element_type=F32) + jnp.dot(pick, low, preferred_element_type=F32)

    def gate(stage):
        if stage == 0:
            send(gl.at[co], gl_r, gg_ss.at[0], gg_rs.at[0], sdev)
        elif stage == 1:
            arrive(gl_r, gg_ss.at[0], gg_rs.at[0], sdev)
            chip = gl[c] + gl_r[...]
            gx[...] = jnp.concatenate([chip[:, :256], chip[:, 256:]], axis=0).astype(BF16)
            send(gx, gx_r, gg_ss.at[1], gg_rs.at[1], xdev)
        elif stage == 2:
            arrive(gx_r, gg_ss.at[1], gg_rs.at[1], xdev)
            gz[z] = (gx[...].astype(F32) + gx_r[...].astype(F32)).astype(BF16)
            for k in PEERS:
                send(gz.at[z], gz.at[z], gg_ss.at[1 + k], gg_rs.at[1 + k], dev(xh, zat(k), c))
        elif stage == 3:
            for k in PEERS:
                zz = zat(-k)
                arrive(gz.at[zz], gg_ss.at[1 + k], gg_rs.at[1 + k], dev(xh, zz, c))
            total = gz[0].astype(F32)
            for zz in range(1, NZ):
                total += gz[zz].astype(F32)
            gg_o[...] = jnp.concatenate([total[:SEQS], total[SEQS:]], axis=1)
            send(gg_o, gg_r, gg_ss.at[9], gg_rs.at[9], sdev)
            gg_v[:, pl.ds(pl.multiple_of(c * HALF, HALF), HALF)] = gg_o[...]
        else:
            arrive(gg_r, gg_ss.at[9], gg_rs.at[9], sdev)
            gg_v[:, pl.ds(pl.multiple_of(co * HALF, HALF), HALF)] = gg_r[...]

    def backward(q):
        cols = slice(q * HALF, (q + 1) * HALF)
        total = jnp.zeros((TOK, HALF), F32)
        for h in range(2):
            rows = wg[h, q * 8:(q + 1) * 8].reshape(HALF, HALF)
            total += lax.dot_general(sc[h], rows, (((1,), (1,)), ((), ())), preferred_element_type=F32)
        pg_v[:, cols] = (total * scaling * slope_v[:, cols]).astype(BF16)

    steps = dict(
        own=own, gz=pass_z, gx=pass_x, tg=token_gates, gelu=gelu, grad=grad, xs=sum_x, rs=sum_z,
        last=last, fin=finish, fwd=forward, gate=gate, bwd=backward,
    )
    for name, *detail in SCHEDULE:
        steps[name](*detail)
    for copy in sent:
        copy.wait_send()


def write_kernel(*refs):
    count = len(refs) // 2
    sources, targets, sems = refs[:count], refs[count:2 * count], refs[-1]
    copies = [pltpu.make_async_copy(a, b, sems.at[i]) for i, (a, b) in enumerate(zip(sources, targets))]
    for copy in copies:
        copy.start()
    for copy in copies:
        copy.wait()


def write_out(*arrays):
    return pl.pallas_call(
        write_kernel,
        out_shape=tuple(jax.ShapeDtypeStruct(a.shape, a.dtype) for a in arrays),
        in_specs=[pl.BlockSpec(memory_space=pl.ANY)] * len(arrays),
        out_specs=tuple(pl.BlockSpec(memory_space=pl.ANY) for _ in arrays),
        scratch_shapes=[pltpu.SemaphoreType.DMA((len(arrays),))],
        name="write_out",
    )(*arrays)


def fused(shift, place, *operands):
    vmem = pltpu.VMEM
    dma = pltpu.SemaphoreType.DMA
    return pl.pallas_call(
        functools.partial(kernel, shift),
        out_shape=(
            jax.ShapeDtypeStruct((TOK, D), BF16),
            jax.ShapeDtypeStruct((TOK, FFW), BF16),
            jax.ShapeDtypeStruct((SEQS, D), F32),
            jax.ShapeDtypeStruct((ROWS, D), F32),
            jax.ShapeDtypeStruct((ROWS, D), F32),
            jax.ShapeDtypeStruct((ROWS, D), F32),
        ),
        in_specs=[pl.BlockSpec(memory_space=pltpu.HBM)] * 9,
        out_specs=[pl.BlockSpec(memory_space=vmem)] * 6,
        scratch_shapes=[
            pltpu.SMEM((1, 1), jnp.int32), vmem((1, TOK), jnp.int32), vmem((SEQS, D), F32),
            vmem((ROWS, D), F32), vmem((ROWS, D), F32), vmem((ROWS, D), F32),
            vmem((TOK, FFW), BF16), vmem((TOK, D), BF16), vmem((TOK, D), BF16),
            vmem((2, 32, ROWS, HALF), BF16),
            vmem((TOK, FFW), BF16), vmem((TOK, FFW), F32),
            vmem((2, NZ, 2, ROWS, TOK), BF16), vmem((2, NZ, ROWS, TOK), BF16),
            vmem((2, TOK, HALF), BF16), vmem((2, TOK, HALF), BF16), vmem((TOK, D), F32),
            vmem((2, 2, NZ, ROWS, HALF), BF16), vmem((24, ROWS, HALF), BF16),
            vmem((NZ, ROWS, HALF), BF16), vmem((ROWS, HALF), BF16),
            vmem((2, SEQS, HALF), F32), vmem((SEQS, HALF), F32),
            vmem((2 * SEQS, HALF // 2), BF16), vmem((2 * SEQS, HALF // 2), BF16),
            vmem((NZ, 2 * SEQS, HALF // 2), BF16), vmem((SEQS, HALF), F32), vmem((SEQS, HALF), F32),
            vmem((2, ROWS, HALF), F32), vmem((2, ROWS, HALF), BF16), vmem((2, ROWS, HALF), BF16),
            dma((9,)),
            dma((24,)), dma((24,)), dma((18,)), dma((18,)), dma((36,)), dma((36,)),
            dma((3,)), dma((3,)), dma((24,)), dma((24,)), dma((9,)), dma((9,)),
            dma((10,)), dma((10,)), dma((2,)), dma((2,)),
        ],
        compiler_params=pltpu.CompilerParams(
            collective_id=place, has_side_effects=True, vmem_limit_bytes=48 << 20
        ),
        name="block_step",
    )(*operands)


def on_device(
    block_input, preact, cotangent, seq_ids, gates, weight, first_moment, second_moment, step
):
    operands = (
        step.reshape(1, 1), pltpu.with_memory_space_constraint(seq_ids, pltpu.HBM), gates[0], weight[0], first_moment[0], second_moment[0],
        preact[0], cotangent[0], block_input[0],
    )
    levels = N_GOSSIP.bit_length() - 1
    branches = [functools.partial(fused, 1 << level, level) for level in range(levels)]
    results = lax.switch(lax.rem(step, levels), branches, *operands)
    return tuple(array[None] for array in write_out(*results))


def solution(mesh):
    split, whole = P("gossip", "fsdp", None), P("gossip", None, None)
    return jax.shard_map(
        on_device,
        mesh=mesh,
        in_specs=(split, split, split, P("gossip", "fsdp"), whole, split, split, split, P()),
        out_specs=(split, split, whole, split, split, split),
        check_vma=False,
    )
```

```python
import functools

import jax
import jax.numpy as jnp
from jax import lax
from jax.experimental import pallas as pl
from jax.experimental.pallas import tpu as pltpu
from jax.sharding import PartitionSpec as P

MESH = pl.DeviceIdType.MESH
BF16, F32 = jnp.bfloat16, jnp.float32

TOK, FFW, D, SEQS = 192, 2048, 1024, 8
ROWS, HALF = 64, 512
NZ = 8
N_GOSSIP = 16

GATHER_HOPS = ((4, 3), (3, 4), (4, 3))
SUM_HOPS = ((3, 4), (4, 3), (3, 4))
X_ORDER = (4, 3, -3, 2, -2, 1, -1, 0)
PEERS = tuple(range(1, NZ))
SCHEDULE = (
    ("own", 0, 0), ("own", 0, 2), ("own", 1, 1), ("own", 1, 2), ("own", 1, 0), ("own", 0, 1), ("gelu", 0), ("tg",),
    ("gz", 0, 0, 1), ("gz", 2, 1, 1), ("grad", 0, 1), ("grad", 1, 1), ("xs", 0), ("gz", 2, 0, 1), ("gx", 0, 0), ("rs", 0, 0, 1),
    ("rs", 0, 1, 1), ("gz", 2, 1, 2), ("gelu", 1), ("gz", 2, 0, 2), ("xs", 1), ("gz", 1, 1, 1), ("gz", 0, 1, 1), ("grad", 1, 0),
    ("xs", 2), ("gz", 0, 0, 2), ("xs", 3), ("gz", 1, 0, 1), ("grad", 0, 0), ("rs", 2, 1, 1), ("gx", 1, 2), ("gz", 2, 0, 3),
    ("rs", 1, 1, 1), ("rs", 1, 0, 1), ("gz", 1, 1, 2), ("gz", 0, 0, 3), ("rs", 0, 1, 2), ("xs", 4), ("gx", 1, 5), ("own", 1, 3),
    ("gz", 2, 1, 3), ("own", 0, 3), ("gz", 2, 0, 4), ("rs", 2, 1, 2), ("gx", 1, 0), ("gz", 0, 1, 2), ("xs", 5), ("rs", 2, 0, 1),
    ("gz", 1, 0, 2), ("xs", 6), ("xs", 7), ("gx", 1, 1), ("gx", 1, 3), ("gz", 1, 1, 3), ("rs", 0, 0, 2), ("rs", 0, 1, 3),
    ("rs", 2, 1, 3), ("gx", 1, 6), ("rs", 1, 0, 2), ("gz", 0, 1, 3), ("gx", 1, 4), ("gx", 1, 7), ("rs", 1, 1, 2),
    ("rs", 2, 0, 2), ("gz", 0, 0, 4), ("rs", 0, 0, 3), ("gz", 1, 1, 4), ("gz", 1, 0, 3), ("fwd", 1), ("rs", 1, 0, 3),
    ("rs", 0, 1, 4), ("fwd", 0), ("rs", 2, 1, 4), ("gate", 0), ("rs", 2, 0, 3), ("gate", 1), ("bwd", 3), ("rs", 1, 0, 4),
    ("rs", 1, 1, 3), ("last", 0), ("last", 2), ("gate", 2), ("bwd", 1), ("bwd", 0), ("bwd", 2), ("last", 1), ("fin", 1),
    ("gate", 3), ("gate", 4), ("fin", 0),
)


def kernel(
    shift,
    step_h, seq_h, gates_h, w_h, m1_h, m2_h, pre_h, cot_h, bi_h,
    bo_v, pg_v, gg_v, wo_v, fo_v, so_v,
    step_ref, seq_ref, gates_ref, w_v, m1_v, m2_v, pre_v, cot_v, bi_v,
    wg, hid, slope_v, ht, hts, sc, scs, tg_v,
    part, rz, rx, rxa,
    gl, gl_r, gx, gx_r, gz, gg_o, gg_r,
    st_v, st_s, st_r,
    lsem,
    agz_s, agz_r, agx_s, agx_r, ags_s, ags_r,
    tok_s, tok_r, rsz_s, rsz_r, rsx_s, rsx_r, gg_ss, gg_rs, go_s, go_r,
):
    g = lax.axis_index("gossip")
    f = lax.axis_index("fsdp")
    xh = lax.div(f, 16)
    z = lax.rem(lax.div(f, 2), NZ)
    c = lax.rem(f, 2)
    xo, co = 1 - xh, 1 - c
    scaling = FFW ** -0.5

    def zat(k):
        return lax.rem(z + (k % NZ), NZ)

    def dev(xx, zz, cc):
        return {"fsdp": xx * 16 + zz * 2 + cc}

    znext = (dev(xh, zat(1), c), dev(xh, zat(-1), c))
    xdev, sdev = dev(xo, z, c), dev(xh, z, co)
    up = {"gossip": lax.rem(g + shift, N_GOSSIP)}
    down = {"gossip": lax.rem(g + N_GOSSIP - shift, N_GOSSIP)}

    sent = []

    def describe(src, dst, ssem, rsem, to):
        return pltpu.make_async_remote_copy(
            src_ref=src, dst_ref=dst, send_sem=ssem, recv_sem=rsem, device_id=to, device_id_type=MESH
        )

    def send(src, dst, ssem, rsem, to):
        copy = describe(src, dst, ssem, rsem, to)
        copy.start()
        sent.append(copy)

    def arrive(dst, ssem, rsem, to):
        describe(dst, dst, ssem, rsem, to).wait_recv()

    loads = {}

    def load(name, src, dst):
        loads[name] = pltpu.make_async_copy(src, dst, lsem.at[len(loads)])
        loads[name].start()

    def need(*wanted):
        for name in wanted:
            if name in loads:
                loads.pop(name).wait()
                waited.append(name)

    waited = []
    load("w", w_h, w_v)
    barrier = pltpu.get_barrier_semaphore()
    greeted = [xdev, sdev, down] + [dev(xh, zat(k), c) for k in PEERS]
    for to in greeted:
        pl.semaphore_signal(barrier, inc=1, device_id=to, device_id_type=MESH)
    rest = (
        ("pre", pre_h, pre_v), ("seq", seq_h, seq_ref), ("gates", gates_h, gates_ref), ("cot", cot_h, cot_v),
        ("bi", bi_h, bi_v), ("step", step_h, step_ref), ("m1", m1_h, m1_v), ("m2", m2_h, m2_v),
    )
    for item in rest:
        load(*item)

    def place(h, xx, zz, cc):
        return wg.at[h, xx * 16 + zz * 2 + cc]

    need("w")
    for h in range(2):
        wg[h, f] = w_v[:, h * HALF:(h + 1) * HALF].astype(BF16)
    pl.semaphore_wait(barrier, len(greeted))

    def send_x(h, j, zz):
        block = place(h, xh, zz, c)
        i = 9 * h + j
        send(block, block, agx_s.at[i], agx_r.at[i], xdev)

    def send_s(h, rel, j, xx, zz):
        block = place(h, xx, zz, c)
        i = 18 * h + 9 * rel + j
        send(block, block, ags_s.at[i], ags_r.at[i], sdev)

    def send_z(stream, way, s, h, xx, zz):
        block = place(h, xx, zz, c)
        i = 8 * stream + 4 * way + s - 1
        send(block, block, agz_s.at[i], agz_r.at[i], znext[way])

    def own(h, link):
        if link < 2:
            send_z(2 * h, link, 1, h, xh, z)
        elif link == 2:
            send_x(h, 0, z)
        else:
            send_s(h, 0, 0, xh, z)

    def pass_z(stream, way, s):
        h, xx, rel = ((0, xh, 0), (0, xo, 1), (1, xh, 0))[stream]
        zz = zat(-s if way == 0 else s)
        i = 8 * stream + 4 * way + s - 1
        arrive(place(h, xx, zz, c), agz_s.at[i], agz_r.at[i], znext[way])
        if s < GATHER_HOPS[stream][way]:
            send_z(stream, way, s + 1, h, xx, zz)
        j = 4 * way + s
        if stream == 2:
            send_x(1, j, zz)
        send_s(h, rel, j, xx, zz)

    def offset(j):
        return 0 if j == 0 else -j if j <= 4 else j - 4

    def pass_x(h, j):
        zz = zat(offset(j))
        i = 9 * h + j
        arrive(place(h, xo, zz, c), agx_s.at[i], agx_r.at[i], xdev)
        if h == 0:
            for way in range(2):
                send_z(1, way, 1, 0, xo, zz)
        send_s(h, 1, j, xo, zz)

    def onehot():
        ids = jnp.broadcast_to(seq_ref[...], (SEQS, TOK))
        return jnp.where(lax.broadcasted_iota(jnp.int32, (SEQS, TOK), 0) == ids, 1.0, 0.0).astype(F32)

    def token_gates():
        need("seq", "gates", "cot")
        gates = gates_ref[...]
        hi = gates.astype(BF16).astype(F32)
        mid = (gates - hi).astype(BF16).astype(F32)
        low = (gates - hi - mid).astype(BF16).astype(F32)
        select = jnp.concatenate([onehot()] * 3, axis=0).T.astype(BF16)
        tg_v[...] = jnp.dot(
            select, jnp.concatenate([hi, mid, low], axis=0).astype(BF16), preferred_element_type=F32
        )
        for h in range(2):
            cols = slice(h * HALF, (h + 1) * HALF)
            sc[h] = (tg_v[:, cols] * cot_v[:, cols].astype(F32)).astype(BF16)
        send(sc, scs, tok_s.at[0], tok_r.at[0], sdev)

    def gelu(which):
        need("pre")
        xx = (xo, xh)[which]

        @pl.loop(0, NZ)
        def _(j):
            cols = pl.ds(pl.multiple_of((xx * NZ + j) * 128, 128), 128)
            u = pre_v[:, cols].astype(F32)
            sq = u * u
            th = jnp.tanh(0.7978845608 * (u + 0.044715 * sq * u))
            slope_v[:, cols] = 0.5 * (1.0 + th) + 0.5 * u * (1.0 - th * th) * 0.7978845608 * (
                1.0 + 3.0 * 0.044715 * sq
            )
            low_hidden = (0.5 * u * (1.0 + th)).astype(BF16)
            hid[:, cols] = low_hidden
            ht[xx, j] = low_hidden.T.reshape(2, ROWS, TOK)

        send(ht.at[xx, :, co], hts.at[xx], tok_s.at[1 + which], tok_r.at[1 + which], sdev)

    def once(key, *how):
        if key not in waited:
            waited.append(key)
            arrive(*how)

    def grad(h, rel):
        xx = (xh, xo)[rel]
        k = 2 - rel
        once("scs", scs, tok_s.at[0], tok_r.at[0], sdev)
        once(("hts", rel), hts.at[xx], tok_s.at[k], tok_r.at[k], sdev)
        mine = ht[xx, :, c].reshape(NZ * ROWS, TOK)
        other = hts[xx].reshape(NZ * ROWS, TOK)
        total = jnp.dot(mine, sc[h], preferred_element_type=F32)
        total += jnp.dot(other, scs[h], preferred_element_type=F32)
        part[h, xx] = (total * scaling).astype(BF16).reshape(NZ, ROWS, HALF)

    def sum_x(j):
        send(part.at[1, xo, zat(X_ORDER[j])], rx.at[j], rsx_s.at[j], rsx_r.at[j], xdev)

    sums = ((0, xo), (0, xh), (1, xh))

    def sum_z(stream, way, s):
        h, xx = sums[stream]
        off = (SUM_HOPS[stream][way] - s + 1) * (1 if way == 0 else -1)
        zz = zat(off)
        block = part.at[h, xx, zz]
        i = 8 * stream + 4 * way + s - 1
        if s > 1 or stream == 2:
            value = block[...].astype(F32)
            if stream == 2:
                jx = X_ORDER.index(4 if off == -4 else off)
                arrive(rx.at[jx], rsx_s.at[jx], rsx_r.at[jx], xdev)
                value += rx[jx].astype(F32)
            if s > 1:
                arrive(rz.at[i - 1], rsz_s.at[i - 1], rsz_r.at[i - 1], znext[way])
                value += rz[i - 1].astype(F32)
            block[...] = value.astype(BF16)
        send(block, rz.at[i], rsz_s.at[i], rsz_r.at[i], znext[way])

    def corrections():
        counter = jnp.full((1, HALF), step_ref[0, 0] + 1, jnp.int32)

        def power(base):
            total, factor = jnp.ones((1, HALF), F32), jnp.full((1, HALF), base, F32)
            for bit in range(7):
                on = jnp.bitwise_and(jnp.right_shift(counter, bit), 1) == 1
                total = jnp.where(on, total * factor, total)
                factor = factor * factor
            return total

        return 1.0 - power(0.9), 1.0 - power(0.999)

    def update(h, total):
        need("step", "m1", "m2")
        corr_first, corr_second = corrections()
        cols = slice(h * HALF, (h + 1) * HALF)
        first = 0.9 * m1_v[:, cols] + 0.1 * total
        second = 0.999 * m2_v[:, cols] + 0.001 * total * total
        fo_v[:, cols], so_v[:, cols] = first, second
        ratio = first / corr_first / (jnp.sqrt(second / corr_second) + 1e-08)
        master = w_v[:, cols]
        stepped = master - 0.01 * (ratio + 0.1 * master)
        st_s[h] = stepped.astype(BF16)
        send(st_s.at[h], st_r.at[h], go_s.at[h], go_r.at[h], up)
        st_v[h] = stepped

    def last(stream):
        h, xx = sums[stream]
        value = part[h, xx, z].astype(F32)
        if stream == 2:
            arrive(rx.at[7], rsx_s.at[7], rsx_r.at[7], xdev)
            value += rx[7].astype(F32)
        for way in range(2):
            i = 8 * stream + 4 * way + SUM_HOPS[stream][way] - 1
            arrive(rz.at[i], rsz_s.at[i], rsz_r.at[i], znext[way])
            value += rz[i].astype(F32)
        if stream == 0:
            part[0, xo, z] = value.astype(BF16)
            send(part.at[0, xo, z], rxa, rsx_s.at[8], rsx_r.at[8], xdev)
            return
        if stream == 1:
            arrive(rxa, rsx_s.at[8], rsx_r.at[8], xdev)
            value += rxa[...].astype(F32)
        update(h, value)

    def finish(h):
        cols = slice(h * HALF, (h + 1) * HALF)
        arrive(st_r.at[h], go_s.at[h], go_r.at[h], up)
        wo_v[:, cols] = 0.5 * (st_v[h] + st_r[h].astype(F32))

    def forward(h):
        for rel, xx, stream in ((0, xh, 2 * h), (1, xo, 1 + h)):
            for j in range(9):
                if j == 0 or (j - 1) % 4 < GATHER_HOPS[stream][(j - 1) // 4]:
                    i = 18 * h + 9 * rel + j
                    arrive(place(h, xx, zat(offset(j)), co), ags_s.at[i], ags_r.at[i], sdev)
        need("bi")
        cols = slice(h * HALF, (h + 1) * HALF)
        projected = jnp.dot(hid[...], wg[h].reshape(FFW, HALF), preferred_element_type=F32) * scaling
        bo_v[:, cols] = (bi_v[:, cols].astype(F32) + tg_v[:, cols] * projected).astype(BF16)
        product = cot_v[:, cols].astype(F32) * projected
        hi = product.astype(BF16)
        low = (product - hi.astype(F32)).astype(BF16)
        pick = onehot().astype(BF16)
        gl[h] = jnp.dot(pick, hi, preferred_element_type=F32) + jnp.dot(pick, low, preferred_element_type=F32)

    def gate(stage):
        if stage == 0:
            send(gl.at[co], gl_r, gg_ss.at[0], gg_rs.at[0], sdev)
        elif stage == 1:
            arrive(gl_r, gg_ss.at[0], gg_rs.at[0], sdev)
            chip = gl[c] + gl_r[...]
            gx[...] = jnp.concatenate([chip[:, :256], chip[:, 256:]], axis=0).astype(BF16)
            send(gx, gx_r, gg_ss.at[1], gg_rs.at[1], xdev)
        elif stage == 2:
            arrive(gx_r, gg_ss.at[1], gg_rs.at[1], xdev)
            gz[z] = (gx[...].astype(F32) + gx_r[...].astype(F32)).astype(BF16)
            for k in PEERS:
                send(gz.at[z], gz.at[z], gg_ss.at[1 + k], gg_rs.at[1 + k], dev(xh, zat(k), c))
        elif stage == 3:
            for k in PEERS:
                zz = zat(-k)
                arrive(gz.at[zz], gg_ss.at[1 + k], gg_rs.at[1 + k], dev(xh, zz, c))
            total = gz[0].astype(F32)
            for zz in range(1, NZ):
                total += gz[zz].astype(F32)
            gg_o[...] = jnp.concatenate([total[:SEQS], total[SEQS:]], axis=1)
            send(gg_o, gg_r, gg_ss.at[9], gg_rs.at[9], sdev)
            gg_v[:, pl.ds(pl.multiple_of(c * HALF, HALF), HALF)] = gg_o[...]
        else:
            arrive(gg_r, gg_ss.at[9], gg_rs.at[9], sdev)
            gg_v[:, pl.ds(pl.multiple_of(co * HALF, HALF), HALF)] = gg_r[...]

    def backward(q):
        cols = slice(q * HALF, (q + 1) * HALF)
        total = jnp.zeros((TOK, HALF), F32)
        for h in range(2):
            rows = wg[h, q * 8:(q + 1) * 8].reshape(HALF, HALF)
            total += lax.dot_general(sc[h], rows, (((1,), (1,)), ((), ())), preferred_element_type=F32)
        pg_v[:, cols] = (total * scaling * slope_v[:, cols]).astype(BF16)

    steps = dict(
        own=own, gz=pass_z, gx=pass_x, tg=token_gates, gelu=gelu, grad=grad, xs=sum_x, rs=sum_z,
        last=last, fin=finish, fwd=forward, gate=gate, bwd=backward,
    )
    for name, *detail in SCHEDULE:
        steps[name](*detail)
    for copy in sent:
        copy.wait_send()


def write_kernel(*refs):
    count = len(refs) // 2
    sources, targets, sems = refs[:count], refs[count:2 * count], refs[-1]
    copies = [pltpu.make_async_copy(a, b, sems.at[i]) for i, (a, b) in enumerate(zip(sources, targets))]
    for copy in copies:
        copy.start()
    for copy in copies:
        copy.wait()


def write_out(*arrays):
    return pl.pallas_call(
        write_kernel,
        out_shape=tuple(jax.ShapeDtypeStruct(a.shape, a.dtype) for a in arrays),
        in_specs=[pl.BlockSpec(memory_space=pl.ANY)] * len(arrays),
        out_specs=tuple(pl.BlockSpec(memory_space=pl.ANY) for _ in arrays),
        scratch_shapes=[pltpu.SemaphoreType.DMA((len(arrays),))],
        name="write_out",
    )(*arrays)


def fused(shift, place, *operands):
    vmem = pltpu.VMEM
    dma = pltpu.SemaphoreType.DMA
    return pl.pallas_call(
        functools.partial(kernel, shift),
        out_shape=(
            jax.ShapeDtypeStruct((TOK, D), BF16),
            jax.ShapeDtypeStruct((TOK, FFW), BF16),
            jax.ShapeDtypeStruct((SEQS, D), F32),
            jax.ShapeDtypeStruct((ROWS, D), F32),
            jax.ShapeDtypeStruct((ROWS, D), F32),
            jax.ShapeDtypeStruct((ROWS, D), F32),
        ),
        in_specs=[pl.BlockSpec(memory_space=pltpu.HBM)] * 9,
        out_specs=[pl.BlockSpec(memory_space=vmem)] * 6,
        scratch_shapes=[
            pltpu.SMEM((1, 1), jnp.int32), vmem((1, TOK), jnp.int32), vmem((SEQS, D), F32),
            vmem((ROWS, D), F32), vmem((ROWS, D), F32), vmem((ROWS, D), F32),
            vmem((TOK, FFW), BF16), vmem((TOK, D), BF16), vmem((TOK, D), BF16),
            vmem((2, 32, ROWS, HALF), BF16),
            vmem((TOK, FFW), BF16), vmem((TOK, FFW), F32),
            vmem((2, NZ, 2, ROWS, TOK), BF16), vmem((2, NZ, ROWS, TOK), BF16),
            vmem((2, TOK, HALF), BF16), vmem((2, TOK, HALF), BF16), vmem((TOK, D), F32),
            vmem((2, 2, NZ, ROWS, HALF), BF16), vmem((24, ROWS, HALF), BF16),
            vmem((NZ, ROWS, HALF), BF16), vmem((ROWS, HALF), BF16),
            vmem((2, SEQS, HALF), F32), vmem((SEQS, HALF), F32),
            vmem((2 * SEQS, HALF // 2), BF16), vmem((2 * SEQS, HALF // 2), BF16),
            vmem((NZ, 2 * SEQS, HALF // 2), BF16), vmem((SEQS, HALF), F32), vmem((SEQS, HALF), F32),
            vmem((2, ROWS, HALF), F32), vmem((2, ROWS, HALF), BF16), vmem((2, ROWS, HALF), BF16),
            dma((9,)),
            dma((24,)), dma((24,)), dma((18,)), dma((18,)), dma((36,)), dma((36,)),
            dma((3,)), dma((3,)), dma((24,)), dma((24,)), dma((9,)), dma((9,)),
            dma((10,)), dma((10,)), dma((2,)), dma((2,)),
        ],
        compiler_params=pltpu.CompilerParams(
            collective_id=place, has_side_effects=True, vmem_limit_bytes=48 << 20
        ),
        name="block_step",
    )(*operands)


def on_device(
    block_input, preact, cotangent, seq_ids, gates, weight, first_moment, second_moment, step
):
    operands = (
        step.reshape(1, 1), pltpu.with_memory_space_constraint(seq_ids, pltpu.HBM), gates[0], weight[0], first_moment[0], second_moment[0],
        preact[0], cotangent[0], block_input[0],
    )
    levels = N_GOSSIP.bit_length() - 1
    branches = [functools.partial(fused, 1 << level, level) for level in range(levels)]
    results = lax.switch(lax.rem(step, levels), branches, *operands)
    return tuple(array[None] for array in write_out(*results))


def solution(mesh):
    split, whole = P("gossip", "fsdp", None), P("gossip", None, None)
    return jax.shard_map(
        on_device,
        mesh=mesh,
        in_specs=(split, split, split, P("gossip", "fsdp"), whole, split, split, split, P()),
        out_specs=(split, split, whole, split, split, split),
        check_vma=False,
    )
```
